256 devices in a mesh: region: 16 (over x, y_lo, core), rows: 16 (over y_hi, z).
Axes of the slice: x: 4, y: 4 (y_hi: 2, y_lo: 2; y = y_hi * 2 + y_lo), z: 8, core: 2. Of those that a mesh axis runs over, the one named last changes fastest.
Arguments:
- basis_values: bfloat16 [393216, 1024], P(('region', 'rows')), may hold values from -6 to 6
- grid_weights: float32 [393216], P(('region', 'rows')), may hold values from 0.0076546553 to 0.07654656
- density_blocks: bfloat16 [131072, 512], P(('region', 'rows')), may hold values from -0.046875 to 0.046875
- pattern: int32 [2048, 8], replicated, may hold values from 0 to 2047, as said below
- active: int32 [256, 16], replicated, may hold values from 0 to 2047, as said below
Outputs:
- density: float32 [393216], P(('region', 'rows'))
- hamiltonian: float32 [131072, 512], P(('region', 'rows'))
The draws below stay inside these ranges and needn't reach their ends.
Inputs may be any that keep to these rules, and one draw needn't show every extreme that they name: `pattern`: block row a names 8 distinct blocks, a itself among them. `active`: block id g lies in region g // 128 and belongs to row index (g // 8) % 16. Batch b lies in region b // 16; its list holds 16 distinct blocks: entries 0 to 7 in its region, the next 4 in the region before it, the last 4 in the region after it (regions counted modulo 16). At most 2 entries of one list belong to one row index, and in every list some row index holds exactly 2.
All inputs are finite; a program needn't handle non-finite values.
Results may differ from the reference program's by a relative error of at most 0.0055.
Values may be sent and summed in bfloat16 or wider, within the bound.
A program may use at most 64 MiB of HBM per device.

```python
import math
import jax
import jax.numpy as jnp
from jax import lax

BS = 64
BLK_DEV = 8
KNZ = 8
ACT_OWN = 8
ACT_SIDE = 4
PTS = 1536
ACT = 16
NBLK = 2048
NB = 131072
BATCHES = 256
POINTS = 393216
N_REGION = 16
N_ROWS = 16


def owner_order(key):
    return jax.random.permutation(jax.random.fold_in(key, 5), N_ROWS).astype(jnp.int32)


def batch_list(subkey, batch_index, order):
    subkeys = jax.random.split(subkey, 5)
    region_here = batch_index // N_ROWS
    rotation = jax.random.randint(subkeys[0], (), 0, N_ROWS, dtype=jnp.int32)
    entry_pos = jnp.arange(ACT, dtype=jnp.int32)
    owners = order[(rotation + jnp.where(entry_pos == 0, 1, entry_pos)) % N_ROWS]
    window = (ACT_OWN - 2) // N_ROWS + 2
    window_start = jax.random.randint(subkeys[1], (), 0, BLK_DEV - window + 1, dtype=jnp.int32)
    own_slot = jnp.where(entry_pos == 0, window_start + window - 1, window_start + (entry_pos - 1) // N_ROWS)
    left_slot = BLK_DEV - 1 - (entry_pos - ACT_OWN) // N_ROWS
    right_slot = (entry_pos - ACT_OWN - ACT_SIDE) // N_ROWS
    is_own = entry_pos < ACT_OWN
    is_left = (entry_pos >= ACT_OWN) & (entry_pos < ACT_OWN + ACT_SIDE)
    slot_index = jnp.where(is_own, own_slot, jnp.where(is_left, left_slot, right_slot))
    offsets = jnp.where(is_own, 0, jnp.where(is_left, N_REGION - 1, 1))
    regions = (region_here + offsets) % N_REGION
    block_ids = (regions * N_ROWS + owners) * BLK_DEV + slot_index
    shuffle_order = jnp.concatenate([jax.random.permutation(subkeys[2], ACT_OWN).astype(jnp.int32), ACT_OWN + jax.random.permutation(subkeys[3], ACT_SIDE).astype(jnp.int32), ACT_OWN + ACT_SIDE + jax.random.permutation(subkeys[4], ACT_SIDE).astype(jnp.int32)])
    return block_ids[shuffle_order].astype(jnp.int32)


def draw_active(key, part):
    order = owner_order(key)
    key = jax.random.fold_in(key, 11)
    batch_count = N_REGION * N_ROWS
    return jax.vmap(batch_list, in_axes=(0, 0, None))(jax.random.split(key, batch_count), jnp.arange(batch_count, dtype=jnp.int32), order)


def pattern_row(subkey, block_index, order, places):
    subkeys = jax.random.split(subkey, 2)
    layers = N_REGION * BLK_DEV
    blocks_region = BLK_DEV * N_ROWS
    layer_here = block_index // blocks_region * BLK_DEV + block_index % BLK_DEV
    owner_here = block_index // BLK_DEV % N_ROWS
    place_here = places[owner_here]
    cands = jnp.arange(3 * N_ROWS, dtype=jnp.int32)
    layer_step = cands // N_ROWS - 1
    offset = cands % N_ROWS
    distance = jnp.where(offset <= N_ROWS // 2, offset, N_ROWS - offset)
    penalty = 2 * distance + 3 * jnp.abs(layer_step)
    jitter = jax.random.randint(subkeys[0], (3 * N_ROWS,), 0, 5, dtype=jnp.int32)
    scores = -(4 * penalty + jitter) * (4 * N_ROWS) + cands
    scores = jnp.where(cands == N_ROWS, -1000000000, scores)
    picked = lax.top_k(scores, KNZ - 1)[1].astype(jnp.int32)
    chosen = jnp.concatenate([jnp.full((1,), N_ROWS, jnp.int32), picked])
    chosen = jax.random.permutation(subkeys[1], chosen).astype(jnp.int32)
    step_chosen = chosen // N_ROWS - 1
    peer_owner = order[(place_here + chosen % N_ROWS) % N_ROWS]
    target_layer = (layer_here + step_chosen) % layers
    return ((target_layer // BLK_DEV * N_ROWS + peer_owner) * BLK_DEV + target_layer % BLK_DEV).astype(jnp.int32)


def draw_pattern(key, part):
    order = owner_order(key)
    places = jnp.argsort(order, stable=True).astype(jnp.int32)
    key = jax.random.fold_in(key, 23)
    return jax.vmap(pattern_row, in_axes=(0, 0, None, None))(jax.random.split(key, NBLK), jnp.arange(NBLK, dtype=jnp.int32), order, places)


def levels(stream_key, dims, cuts, low, top_value):
    level, own = 1.0, jax.random.fold_in(stream_key, 6)
    for dim, shards_of in cuts:
        heights = jnp.exp(jax.random.uniform(jax.random.fold_in(own, dim), (shards_of,), jnp.float32, low / len(cuts), top_value / len(cuts)))
        level = level * jnp.repeat(heights, dims[dim] // shards_of).reshape([-1 if axis == dim else 1 for axis in range(len(dims))])
    return level


def centred(key, shape, scale, bound, cuts=(), kind=jnp.bfloat16):
    factor_of = levels(key, shape, cuts, -0.22, 0.18) if cuts else 1.0
    values = jax.random.normal(key, shape, jnp.float32) * scale * factor_of
    return jnp.minimum(jnp.maximum(values, -bound), bound).astype(kind)


def setup_inputs(seed: int = 0) -> dict:
    streams_of = jax.random.split(jax.random.key(seed), 6)
    basis_values = centred(streams_of[0], (POINTS, ACT * BS), 1.0, 6.0, ((0, 256),))
    grid_weights = jnp.clip(jnp.exp(math.log(0.07654656) - 2.3025852 * jax.random.uniform(streams_of[1], (POINTS,), jnp.float32) ** levels(streams_of[1], (POINTS,), ((0, 256),), -0.2, 0.2)), 0.0076546553, 0.07654656)
    density_blocks = centred(streams_of[2], (NB, KNZ * BS), 0.003, 0.046875, ((0, 256),))
    pattern = draw_pattern(jax.random.fold_in(streams_of[5], 71), 0)
    active = draw_active(jax.random.fold_in(streams_of[5], 71), 0)
    return dict(basis_values=basis_values, grid_weights=grid_weights, density_blocks=density_blocks, pattern=pattern, active=active)


def reference(basis_values, grid_weights, density_blocks, pattern, active):
    row_width = KNZ * BS
    stored = density_blocks.reshape(NBLK, BS, row_width)
    values = basis_values.reshape(BATCHES, PTS, ACT * BS)
    weights = grid_weights.reshape(BATCHES, PTS)

    def one_batch(totals, inputs):
        basis_rows, point_weights, block_ids = inputs
        column_ids = pattern[block_ids]
        matches = (column_ids[:, :, None] == block_ids[None, None, :]).astype(jnp.float32)
        row_blocks = stored[block_ids].astype(jnp.float32).reshape(ACT, BS, KNZ, BS)
        sub_density = jnp.einsum("krmc,kmj->krjc", row_blocks, matches)
        sub_density = sub_density.astype(jnp.bfloat16).reshape(ACT * BS, ACT * BS)
        product = jnp.dot(basis_rows, sub_density, preferred_element_type=jnp.float32)
        density = jnp.sum(product * basis_rows.astype(jnp.float32), axis=1)
        scaled = (basis_rows.astype(jnp.float32) * (point_weights * jnp.tanh(density))[:, None]).astype(jnp.bfloat16)
        batch_ham = jnp.dot(scaled.T, basis_rows, preferred_element_type=jnp.float32).astype(jnp.bfloat16)
        ham_blocks = batch_ham.astype(jnp.float32).reshape(ACT, BS, ACT, BS)
        kept_blocks = jnp.einsum("krjc,kmj->krmc", ham_blocks, matches).reshape(ACT, BS, row_width)
        return totals.at[block_ids].add(kept_blocks), density

    start_totals = jnp.zeros((NBLK, BS, row_width), jnp.float32)
    totals, density = lax.scan(one_batch, start_totals, (values, weights, active))
    return density.reshape(BATCHES * PTS), totals.reshape(NB, row_width)
```

```python
import functools

import jax
import jax.numpy as jnp
from jax import lax
from jax.experimental import pallas as pl
from jax.experimental.pallas import tpu as pltpu
from jax.sharding import PartitionSpec as P

BS = 64
BLK_DEV = 8
KNZ = 8
ACT = 16
PTS = 1536
ROWS = 16
WIDTH = KNZ * BS
COLS = ACT * BS
CHUNK = 256
MESH = pl.DeviceIdType.MESH
F32 = jnp.float32
BF16 = jnp.bfloat16
PEERS = tuple(
    (dy, dz)
    for dz in (4, 3, 5, 2, 6, 1, 7, 0)
    for dy in (0, 1)
    if (dy, dz) != (0, 0)
)


def half_masks():
    lane = lax.broadcasted_iota(jnp.int32, (BS, 128), 1)
    low = jnp.where(lane < BS, 1.0, 0.0).astype(BF16)
    high = jnp.where(lane < BS, 0.0, 1.0).astype(BF16)
    return low, high


def pair_of_blocks(source, row, first, second, masks):
    low, high = masks
    a = source[first & 1, row, first >> 1]
    b = source[1 - (second & 1), row, second >> 1]
    return a * low + b * high


def swap_halves(values):
    return pltpu.roll(values, 64, 1)


def kernel(
    act, pat, weights, x_hbm, d_hbm,
    dens_out, ham_out,
    xv, xt, ext, send_d, recv_d, rows2, dfull, svec, hrows, send_h, recv_h,
    halo_out, halo_in,
    tab_row, tab_arr, tab_m, tab_j, tab_slot,
    local_sems, halo_send, halo_recv, a2a_send, a2a_recv,
):
    g = lax.axis_index("region")
    me = lax.axis_index("rows")
    y = lax.div(me, 8)
    z = lax.rem(me, 8)
    left, right = lax.rem(g + 15, 16), lax.rem(g + 1, 16)

    def peer(dy, dz):
        return lax.rem(y + dy, 2) * 8 + lax.rem(z + dz, 8)

    x_copy = pltpu.make_async_copy(x_hbm, xv, local_sems.at[0])
    x_copy.start()
    d_copy = pltpu.make_async_copy(d_hbm, ext.at[pl.ds(BLK_DEV, BLK_DEV)], local_sems.at[1])
    d_copy.start()

    barrier = pltpu.get_barrier_semaphore()
    for n in (left, right):
        pl.semaphore_signal(barrier, inc=1, device_id=(n, me), device_id_type=MESH)
    for dy, dz in PEERS:
        pl.semaphore_signal(barrier, inc=1, device_id=(g, peer(dy, dz)), device_id_type=MESH)
    pl.semaphore_wait(barrier, 17)

    to_right = pltpu.make_async_remote_copy(
        d_hbm, ext.at[pl.ds(0, BLK_DEV)], halo_send.at[0], halo_recv.at[0],
        device_id=(right, me), device_id_type=MESH)
    to_left = pltpu.make_async_remote_copy(
        d_hbm, ext.at[pl.ds(2 * BLK_DEV, BLK_DEV)], halo_send.at[1], halo_recv.at[1],
        device_id=(left, me), device_id_type=MESH)
    to_right.start()
    to_left.start()

    def rows_of_batch(b, carry):
        first = jnp.int32(0)
        second = jnp.int32(0)
        count = jnp.int32(0)
        for e in range(ACT):
            block = act[e, g * ROWS + b]
            mine = ((block >> 3) & (ROWS - 1)) == me
            row = jnp.minimum(((block >> 7) - g + 1) & 15, 2) * BLK_DEV + (block & 7)
            first = jnp.where(mine & (count == 0), row, first)
            second = jnp.where(mine & (count == 1), row, second)
            count = count + mine.astype(jnp.int32)
        tab_row[2 * b] = first
        tab_row[2 * b + 1] = second
        tab_row[2 * ROWS + b] = count
        return carry

    lax.fori_loop(0, ROWS, rows_of_batch, 0)

    d_copy.wait()
    to_right.wait_recv()
    to_left.wait_recv()

    first_copies = []
    for i, (dy, dz) in enumerate(PEERS):
        p = peer(dy, dz)
        for c in range(2):
            send_d[p, c] = ext[tab_row[2 * p + c]]
        copy = pltpu.make_async_remote_copy(
            send_d.at[p], recv_d.at[pl.ds(2 * me, 2)], a2a_send.at[i], a2a_recv.at[i],
            device_id=(g, p), device_id_type=MESH)
        copy.start()
        first_copies.append(copy)
    for c in range(2):
        recv_d[2 * me + c] = ext[tab_row[2 * me + c]]

    ids = [act[k, g * ROWS + me] for k in range(ACT)]
    owners = [(i >> 3) & (ROWS - 1) for i in ids]
    for k in range(ACT):
        earlier = jnp.int32(0)
        for j in range(k):
            earlier = earlier + (owners[j] == owners[k]).astype(jnp.int32)
        tab_arr[k] = owners[k] * 2 + jnp.minimum(earlier, 1)

    def slot_entries(s, carry):
        entry = jnp.int32(0)
        for k in range(ACT):
            entry = jnp.where(tab_arr[k] == s, k, entry)
        tab_slot[s] = entry
        return carry

    lax.fori_loop(0, 2 * ROWS, slot_entries, 0)

    def match_row(k, carry):
        block = act[k, g * ROWS + me]
        found_m = [jnp.int32(KNZ)] * ACT
        for m in range(KNZ):
            column = pat[m, block]
            found = jnp.int32(ACT)
            for j in range(ACT):
                same = column == act[j, g * ROWS + me]
                found = jnp.where(same, j, found)
                found_m[j] = jnp.where(same, m, found_m[j])
            tab_j[k * KNZ + m] = found
        for j in range(ACT):
            tab_m[k * ACT + j] = found_m[j]
        return carry

    lax.fori_loop(0, ACT, match_row, 0)

    rows2[:, :, KNZ // 2] = jnp.zeros((2, ACT, BS, 128), BF16)
    hrows[:, :, ACT // 2] = jnp.zeros((2, ACT, BS, 128), BF16)
    recv_h[:, 2] = jnp.zeros((ROWS, BS, WIDTH), BF16)

    x_copy.wait()

    def transpose_chunk(i, carry):
        points = pl.ds(pl.multiple_of(i * 128, 128), 128)
        xt[:, points] = jnp.transpose(xv[points, :])
        return carry

    lax.fori_loop(0, PTS // 128, transpose_chunk, 0)

    masks = half_masks()
    for copy in first_copies:
        copy.wait_recv()

    def spread_row(k, carry):
        row = recv_d[tab_arr[k]]
        for q in range(KNZ // 2):
            part = row[:, q * 128 : (q + 1) * 128]
            rows2[0, k, q] = part
            rows2[1, k, q] = swap_halves(part.astype(F32)).astype(BF16)
        for q in range(ACT // 2):
            first = tab_m[k * ACT + 2 * q]
            second = tab_m[k * ACT + 2 * q + 1]
            dfull[pl.ds(pl.multiple_of(k * BS, BS), BS), q * 128 : (q + 1) * 128] = pair_of_blocks(
                rows2, k, first, second, masks)
        return carry

    lax.fori_loop(0, ACT, spread_row, 0)

    def density_chunk(i, carry):
        points = pl.ds(pl.multiple_of(i * CHUNK, CHUNK), CHUNK)
        x = xv[points, :]
        part = jnp.zeros((CHUNK, 128), F32)
        for n in range(COLS // CHUNK):
            product = jnp.dot(x, dfull[:, n * CHUNK : (n + 1) * CHUNK], preferred_element_type=F32)
            product = product * x[:, n * CHUNK : (n + 1) * CHUNK].astype(F32)
            part = part + (product[:, :128] + product[:, 128:])
        dens = jnp.sum(jnp.transpose(part), axis=0, keepdims=True)
        dens_out[:, points] = dens
        svec[:, points] = weights[:, points] * jnp.tanh(dens)
        return carry

    lax.fori_loop(0, PTS // CHUNK, density_chunk, 0)

    def ham_chunk(i, carry):
        scaled = (xt[pl.ds(pl.multiple_of(i * CHUNK, CHUNK), CHUNK), :].astype(F32) * svec[...]).astype(BF16)
        for n in range(COLS // CHUNK):
            block = jnp.dot(scaled, xv[:, n * CHUNK : (n + 1) * CHUNK], preferred_element_type=F32)
            for half in range(CHUNK // 128):
                part = block[:, half * 128 : (half + 1) * 128]
                swapped = swap_halves(part).astype(BF16)
                part = part.astype(BF16)
                for kk in range(CHUNK // BS):
                    entry = i * (CHUNK // BS) + kk
                    hrows[0, entry, 2 * n + half] = part[kk * BS : (kk + 1) * BS]
                    hrows[1, entry, 2 * n + half] = swapped[kk * BS : (kk + 1) * BS]
        return carry

    lax.fori_loop(0, COLS // CHUNK, ham_chunk, 0)

    for copy in first_copies:
        copy.wait_send()

    def gather_slots(p, target, target_row):
        for c in range(2):
            k = tab_slot[2 * p + c]
            for q in range(KNZ // 2):
                first = tab_j[k * KNZ + 2 * q]
                second = tab_j[k * KNZ + 2 * q + 1]
                target[target_row, c, :, q * 128 : (q + 1) * 128] = pair_of_blocks(
                    hrows, k, first, second, masks)

    second_copies = []
    for i, (dy, dz) in enumerate(PEERS):
        p = peer(dy, dz)
        gather_slots(p, send_h, p)
        copy = pltpu.make_async_remote_copy(
            send_h.at[p], recv_h.at[me, pl.ds(0, 2)], a2a_send.at[15 + i], a2a_recv.at[15 + i],
            device_id=(g, p), device_id_type=MESH)
        copy.start()
        second_copies.append(copy)
    gather_slots(me, recv_h, me)
    for copy in second_copies:
        copy.wait_recv()

    def sum_row(t):
        picks = []
        for b in range(ROWS):
            count = tab_row[2 * ROWS + b]
            picks.append(jnp.where(
                (tab_row[2 * b] == t) & (count > 0), 0,
                jnp.where((tab_row[2 * b + 1] == t) & (count > 1), 1, 2)))
        total = recv_h[0, picks[0]].astype(F32)
        for b in range(1, ROWS):
            total = total + recv_h[b, picks[b]].astype(F32)
        return total

    def side_row(t, carry):
        for side, base in ((0, 0), (1, 2 * BLK_DEV)):
            halo_out[side, t] = sum_row(base + t).astype(BF16)
        return carry

    lax.fori_loop(0, BLK_DEV, side_row, 0)

    back_left = pltpu.make_async_remote_copy(
        halo_out.at[0], halo_in.at[0], halo_send.at[2], halo_recv.at[2],
        device_id=(left, me), device_id_type=MESH)
    back_right = pltpu.make_async_remote_copy(
        halo_out.at[1], halo_in.at[1], halo_send.at[3], halo_recv.at[3],
        device_id=(right, me), device_id_type=MESH)
    back_left.start()
    back_right.start()

    def own_row(t, carry):
        ham_out[t] = sum_row(BLK_DEV + t)
        return carry

    lax.fori_loop(0, BLK_DEV, own_row, 0)
    back_left.wait_recv()
    back_right.wait_recv()

    def add_row(t, carry):
        ham_out[t] = ham_out[t] + halo_in[0, t].astype(F32) + halo_in[1, t].astype(F32)
        return carry

    lax.fori_loop(0, BLK_DEV, add_row, 0)

    for copy in second_copies:
        copy.wait_send()
    for copy in (to_right, to_left, back_left, back_right):
        copy.wait_send()


def shards(basis_values, grid_weights, density_blocks, pattern, active):
    vmem = pl.BlockSpec(memory_space=pltpu.VMEM)
    smem = pl.BlockSpec(memory_space=pltpu.SMEM)
    hbm = pl.BlockSpec(memory_space=pl.ANY)
    dens, ham = pl.pallas_call(
        kernel,
        out_shape=(
            jax.ShapeDtypeStruct((1, PTS), F32),
            jax.ShapeDtypeStruct((BLK_DEV, BS, WIDTH), F32),
        ),
        in_specs=[smem, smem, vmem, hbm, hbm],
        out_specs=(vmem, vmem),
        scratch_shapes=[
            pltpu.VMEM((PTS, COLS), BF16),
            pltpu.VMEM((COLS, PTS), BF16),
            pltpu.VMEM((3 * BLK_DEV, BS, WIDTH), BF16),
            pltpu.VMEM((ROWS, 2, BS, WIDTH), BF16),
            pltpu.VMEM((2 * ROWS, BS, WIDTH), BF16),
            pltpu.VMEM((2, ACT, KNZ // 2 + 1, BS, 128), BF16),
            pltpu.VMEM((COLS, COLS), BF16),
            pltpu.VMEM((1, PTS), F32),
            pltpu.VMEM((2, ACT, ACT // 2 + 1, BS, 128), BF16),
            pltpu.VMEM((ROWS, 2, BS, WIDTH), BF16),
            pltpu.VMEM((ROWS, 3, BS, WIDTH), BF16),
            pltpu.VMEM((2, BLK_DEV, BS, WIDTH), BF16),
            pltpu.VMEM((2, BLK_DEV, BS, WIDTH), BF16),
            pltpu.SMEM((3 * ROWS,), jnp.int32),
            pltpu.SMEM((ACT,), jnp.int32),
            pltpu.SMEM((ACT * ACT,), jnp.int32),
            pltpu.SMEM((ACT * KNZ,), jnp.int32),
            pltpu.SMEM((2 * ROWS,), jnp.int32),
            pltpu.SemaphoreType.DMA((2,)),
            pltpu.SemaphoreType.DMA((4,)),
            pltpu.SemaphoreType.DMA((4,)),
            pltpu.SemaphoreType.DMA((30,)),
            pltpu.SemaphoreType.DMA((30,)),
        ],
        compiler_params=pltpu.CompilerParams(
            collective_id=0, has_side_effects=True, vmem_limit_bytes=56 << 20
        ),
    )(
        active.T,
        pattern.T,
        grid_weights.reshape(1, PTS),
        basis_values,
        density_blocks.reshape(BLK_DEV, BS, WIDTH),
    )
    return dens.reshape(PTS), ham.reshape(BLK_DEV * BS, WIDTH)


def solution(mesh):
    placed = (
        P(("region", "rows"), None),
        P(("region", "rows")),
        P(("region", "rows"), None),
        P(),
        P(),
    )
    return jax.shard_map(
        shards,
        mesh=mesh,
        in_specs=placed,
        out_specs=(P(("region", "rows")), P(("region", "rows"), None)),
        check_vma=False,
    )
```

```python
import functools

import jax
import jax.numpy as jnp
from jax import lax
from jax.experimental import pallas as pl
from jax.experimental.pallas import tpu as pltpu
from jax.sharding import PartitionSpec as P

BS = 64
BLK_DEV = 8
KNZ = 8
ACT = 16
PTS = 1536
ROWS = 16
WIDTH = KNZ * BS
COLS = ACT * BS
CHUNK = 256
HALO = 2
MESH = pl.DeviceIdType.MESH
F32 = jnp.float32
BF16 = jnp.bfloat16
PEERS = tuple(
    (dy, dz)
    for dz in (4, 3, 5, 2, 6, 1, 7, 0)
    for dy in (0, 1)
    if (dy, dz) != (0, 0)
)


def half_masks():
    lane = lax.broadcasted_iota(jnp.int32, (BS, 128), 1)
    low = jnp.where(lane < BS, 1.0, 0.0).astype(BF16)
    high = jnp.where(lane < BS, 0.0, 1.0).astype(BF16)
    return low, high


def two_blocks(source, row_a, block_a, row_b, block_b, masks):
    low, high = masks
    a = source[block_a & 1, row_a, block_a >> 1]
    b = source[1 - (block_b & 1), row_b, block_b >> 1]
    return a * low + b * high


def pair_of_blocks(source, row, first, second, masks):
    return two_blocks(source, row, first, row, second, masks)


def swap_halves(values):
    return pltpu.roll(values, 64, 1)


def keep_both(target, row, part, values):
    target[0, row, part] = values
    target[1, row, part] = swap_halves(values.astype(F32)).astype(BF16)


def full_kernel(
    act, pat, weights, x_hbm, d_hbm,
    dens_out, ham_out,
    xv, xt, ext, send_d, recv_d, rows2, dfull, svec, hrows, send_h, recv_h,
    halo_out, halo_in,
    tab_row, tab_arr, tab_m, tab_j, tab_slot,
    local_sems, halo_send, halo_recv, a2a_send, a2a_recv,
):
    g = lax.axis_index("region")
    me = lax.axis_index("rows")
    y = lax.div(me, 8)
    z = lax.rem(me, 8)
    left, right = lax.rem(g + 15, 16), lax.rem(g + 1, 16)

    def peer(dy, dz):
        return lax.rem(y + dy, 2) * 8 + lax.rem(z + dz, 8)

    x_copy = pltpu.make_async_copy(x_hbm, xv, local_sems.at[0])
    x_copy.start()
    d_copy = pltpu.make_async_copy(d_hbm, ext.at[pl.ds(BLK_DEV, BLK_DEV)], local_sems.at[1])
    d_copy.start()

    barrier = pltpu.get_barrier_semaphore()
    for n in (left, right):
        pl.semaphore_signal(barrier, inc=1, device_id=(n, me), device_id_type=MESH)
    for dy, dz in PEERS:
        pl.semaphore_signal(barrier, inc=1, device_id=(g, peer(dy, dz)), device_id_type=MESH)
    pl.semaphore_wait(barrier, 17)

    to_right = pltpu.make_async_remote_copy(
        d_hbm, ext.at[pl.ds(0, BLK_DEV)], halo_send.at[0], halo_recv.at[0],
        device_id=(right, me), device_id_type=MESH)
    to_left = pltpu.make_async_remote_copy(
        d_hbm, ext.at[pl.ds(2 * BLK_DEV, BLK_DEV)], halo_send.at[1], halo_recv.at[1],
        device_id=(left, me), device_id_type=MESH)
    to_right.start()
    to_left.start()

    def rows_of_batch(b, carry):
        first = jnp.int32(0)
        second = jnp.int32(0)
        count = jnp.int32(0)
        for e in range(ACT):
            block = act[e, g * ROWS + b]
            mine = ((block >> 3) & (ROWS - 1)) == me
            row = jnp.minimum(((block >> 7) - g + 1) & 15, 2) * BLK_DEV + (block & 7)
            first = jnp.where(mine & (count == 0), row, first)
            second = jnp.where(mine & (count == 1), row, second)
            count = count + mine.astype(jnp.int32)
        tab_row[2 * b] = first
        tab_row[2 * b + 1] = second
        tab_row[2 * ROWS + b] = count
        return carry

    lax.fori_loop(0, ROWS, rows_of_batch, 0)

    d_copy.wait()
    to_right.wait_recv()
    to_left.wait_recv()

    first_copies = []
    for i, (dy, dz) in enumerate(PEERS):
        p = peer(dy, dz)
        for c in range(2):
            send_d[p, c] = ext[tab_row[2 * p + c]]
        copy = pltpu.make_async_remote_copy(
            send_d.at[p], recv_d.at[pl.ds(2 * me, 2)], a2a_send.at[i], a2a_recv.at[i],
            device_id=(g, p), device_id_type=MESH)
        copy.start()
        first_copies.append(copy)
    for c in range(2):
        recv_d[2 * me + c] = ext[tab_row[2 * me + c]]

    ids = [act[k, g * ROWS + me] for k in range(ACT)]
    owners = [(i >> 3) & (ROWS - 1) for i in ids]
    for k in range(ACT):
        earlier = jnp.int32(0)
        for j in range(k):
            earlier = earlier + (owners[j] == owners[k]).astype(jnp.int32)
        tab_arr[k] = owners[k] * 2 + jnp.minimum(earlier, 1)

    def slot_entries(s, carry):
        entry = jnp.int32(0)
        for k in range(ACT):
            entry = jnp.where(tab_arr[k] == s, k, entry)
        tab_slot[s] = entry
        return carry

    lax.fori_loop(0, 2 * ROWS, slot_entries, 0)

    def match_row(k, carry):
        block = act[k, g * ROWS + me]
        found_m = [jnp.int32(KNZ)] * ACT
        for m in range(KNZ):
            column = pat[m, block]
            found = jnp.int32(ACT)
            for j in range(ACT):
                same = column == act[j, g * ROWS + me]
                found = jnp.where(same, j, found)
                found_m[j] = jnp.where(same, m, found_m[j])
            tab_j[k * KNZ + m] = found
        for j in range(ACT):
            tab_m[k * ACT + j] = found_m[j]
        return carry

    lax.fori_loop(0, ACT, match_row, 0)

    rows2[:, :, KNZ // 2] = jnp.zeros((2, ACT, BS, 128), BF16)
    hrows[:, :, ACT // 2] = jnp.zeros((2, ACT, BS, 128), BF16)
    recv_h[:, 2] = jnp.zeros((ROWS, BS, WIDTH), BF16)

    x_copy.wait()

    def transpose_chunk(i, carry):
        points = pl.ds(pl.multiple_of(i * 128, 128), 128)
        xt[:, points] = jnp.transpose(xv[points, :])
        return carry

    lax.fori_loop(0, PTS // 128, transpose_chunk, 0)

    masks = half_masks()
    for copy in first_copies:
        copy.wait_recv()

    def spread_row(k, carry):
        row = recv_d[tab_arr[k]]
        for q in range(KNZ // 2):
            part = row[:, q * 128 : (q + 1) * 128]
            rows2[0, k, q] = part
            rows2[1, k, q] = swap_halves(part.astype(F32)).astype(BF16)
        for q in range(ACT // 2):
            first = tab_m[k * ACT + 2 * q]
            second = tab_m[k * ACT + 2 * q + 1]
            dfull[pl.ds(pl.multiple_of(k * BS, BS), BS), q * 128 : (q + 1) * 128] = pair_of_blocks(
                rows2, k, first, second, masks)
        return carry

    lax.fori_loop(0, ACT, spread_row, 0)

    def density_chunk(i, carry):
        points = pl.ds(pl.multiple_of(i * CHUNK, CHUNK), CHUNK)
        x = xv[points, :]
        part = jnp.zeros((CHUNK, 128), F32)
        for n in range(COLS // CHUNK):
            product = jnp.dot(x, dfull[:, n * CHUNK : (n + 1) * CHUNK], preferred_element_type=F32)
            product = product * x[:, n * CHUNK : (n + 1) * CHUNK].astype(F32)
            part = part + (product[:, :128] + product[:, 128:])
        dens = jnp.sum(jnp.transpose(part), axis=0, keepdims=True)
        dens_out[:, points] = dens
        svec[:, points] = weights[:, points] * jnp.tanh(dens)
        return carry

    lax.fori_loop(0, PTS // CHUNK, density_chunk, 0)

    def ham_chunk(i, carry):
        scaled = (xt[pl.ds(pl.multiple_of(i * CHUNK, CHUNK), CHUNK), :].astype(F32) * svec[...]).astype(BF16)
        for n in range(COLS // CHUNK):
            block = jnp.dot(scaled, xv[:, n * CHUNK : (n + 1) * CHUNK], preferred_element_type=F32)
            for half in range(CHUNK // 128):
                part = block[:, half * 128 : (half + 1) * 128]
                swapped = swap_halves(part).astype(BF16)
                part = part.astype(BF16)
                for kk in range(CHUNK // BS):
                    entry = i * (CHUNK // BS) + kk
                    hrows[0, entry, 2 * n + half] = part[kk * BS : (kk + 1) * BS]
                    hrows[1, entry, 2 * n + half] = swapped[kk * BS : (kk + 1) * BS]
        return carry

    lax.fori_loop(0, COLS // CHUNK, ham_chunk, 0)

    for copy in first_copies:
        copy.wait_send()

    def gather_slots(p, target, target_row):
        for c in range(2):
            k = tab_slot[2 * p + c]
            for q in range(KNZ // 2):
                first = tab_j[k * KNZ + 2 * q]
                second = tab_j[k * KNZ + 2 * q + 1]
                target[target_row, c, :, q * 128 : (q + 1) * 128] = pair_of_blocks(
                    hrows, k, first, second, masks)

    second_copies = []
    for i, (dy, dz) in enumerate(PEERS):
        p = peer(dy, dz)
        gather_slots(p, send_h, p)
        copy = pltpu.make_async_remote_copy(
            send_h.at[p], recv_h.at[me, pl.ds(0, 2)], a2a_send.at[15 + i], a2a_recv.at[15 + i],
            device_id=(g, p), device_id_type=MESH)
        copy.start()
        second_copies.append(copy)
    gather_slots(me, recv_h, me)
    for copy in second_copies:
        copy.wait_recv()

    def sum_row(t):
        picks = []
        for b in range(ROWS):
            count = tab_row[2 * ROWS + b]
            picks.append(jnp.where(
                (tab_row[2 * b] == t) & (count > 0), 0,
                jnp.where((tab_row[2 * b + 1] == t) & (count > 1), 1, 2)))
        total = recv_h[0, picks[0]].astype(F32)
        for b in range(1, ROWS):
            total = total + recv_h[b, picks[b]].astype(F32)
        return total

    def side_row(t, carry):
        for side, base in ((0, 0), (1, 2 * BLK_DEV)):
            halo_out[side, t] = sum_row(base + t).astype(BF16)
        return carry

    lax.fori_loop(0, BLK_DEV, side_row, 0)

    back_left = pltpu.make_async_remote_copy(
        halo_out.at[0], halo_in.at[0], halo_send.at[2], halo_recv.at[2],
        device_id=(left, me), device_id_type=MESH)
    back_right = pltpu.make_async_remote_copy(
        halo_out.at[1], halo_in.at[1], halo_send.at[3], halo_recv.at[3],
        device_id=(right, me), device_id_type=MESH)
    back_left.start()
    back_right.start()

    def own_row(t, carry):
        ham_out[t] = sum_row(BLK_DEV + t)
        return carry

    lax.fori_loop(0, BLK_DEV, own_row, 0)
    back_left.wait_recv()
    back_right.wait_recv()

    def add_row(t, carry):
        ham_out[t] = ham_out[t] + halo_in[0, t].astype(F32) + halo_in[1, t].astype(F32)
        return carry

    lax.fori_loop(0, BLK_DEV, add_row, 0)

    for copy in second_copies:
        copy.wait_send()
    for copy in (to_right, to_left, back_left, back_right):
        copy.wait_send()


def offset_of(i):
    j = lax.div(i, 2)
    dz = 4 + lax.div(j + 1, 2) * (1 - 2 * lax.rem(j, 2))
    return 1 - lax.rem(i, 2), dz


def packed_kernel(
    act, pat, weights, x_hbm, d_hbm,
    dens_out, ham_out, flag_out,
    xv, xt, own, halo_d, ext2, send_d, recv_d, rows2, dfull, svec, hrows, send_h,
    recv_h, hvar, expanded, halo_out, halo_in, row_flags, region_flags,
    halo_src, row_map, back_map, tab_row, tab_src, tab_pos,
    tab_j, tab_rank, tab_local, tab_q, tab_start, tab_owner, tab_dpos, tab_h,
    local_sems, halo_send, halo_recv, a2a_send, a2a_recv, flag_send, flag_recv,
):
    g = lax.axis_index("region")
    me = lax.axis_index("rows")
    y = lax.div(me, 8)
    z = lax.rem(me, 8)
    left, right = lax.rem(g + 15, 16), lax.rem(g + 1, 16)

    def peer(i):
        dy, dz = offset_of(i)
        return lax.rem(y + dy, 2) * 8 + lax.rem(z + dz, 8)

    def sender(i):
        dy, dz = offset_of(i)
        return lax.rem(y + dy, 2) * 8 + lax.rem(z + 8 - dz, 8)

    x_copy = pltpu.make_async_copy(x_hbm, xv, local_sems.at[0])
    d_copy = pltpu.make_async_copy(d_hbm, own, local_sems.at[1])
    d_copy.start()
    x_copy.start()

    barrier = pltpu.get_barrier_semaphore()
    for n in (left, right) + tuple(lax.rem(g + 16 - hop, 16) for hop in (2, 4, 8)):
        pl.semaphore_signal(barrier, inc=1, device_id=(n, me), device_id_type=MESH)

    def greet(i, carry):
        pl.semaphore_signal(barrier, inc=1, device_id=(g, peer(i)), device_id_type=MESH)
        return carry

    lax.fori_loop(0, ROWS - 1, greet, 0)

    def named(region, start):
        def one(b, mask):
            for e in range(start, start + 4):
                block = act[e, region * ROWS + b]
                bit = (1 + (block & 1)) * (1 + 3 * ((block >> 1) & 1)) * (1 + 15 * ((block >> 2) & 1))
                mask = mask | jnp.where(((block >> 3) & (ROWS - 1)) == me, bit, 0)
            return mask

        return lax.fori_loop(0, ROWS, one, jnp.int32(0))

    def ranks(mask):
        taken = jnp.int32(0)
        bits, places = [], []
        for s in range(BLK_DEV):
            bit = (mask >> s) & 1
            bits.append(bit)
            places.append(taken)
            taken = taken + bit
        return bits, places, taken

    overflow = jnp.int32(0)
    for side, mask in enumerate((named(right, 8), named(left, 12))):
        bits, places, taken = ranks(mask)
        for i in range(HALO):
            source = jnp.int32(0)
            for s in range(BLK_DEV):
                source = jnp.where((bits[s] == 1) & (places[s] == i), s, source)
            halo_src[side * HALO + i] = source
        for s in range(BLK_DEV):
            back_map[side * BLK_DEV + s] = jnp.where(bits[s] == 1, jnp.minimum(places[s], HALO - 1), HALO)
        overflow = jnp.maximum(overflow, (taken > HALO).astype(jnp.int32))

    d_copy.wait()
    for side in range(2):
        for i in range(HALO):
            halo_out[side, i] = own[halo_src[side * HALO + i]]
    pl.semaphore_wait(barrier, 20)

    to_right = pltpu.make_async_remote_copy(
        halo_out.at[0], halo_d.at[0], halo_send.at[0], halo_recv.at[0],
        device_id=(right, me), device_id_type=MESH)
    to_left = pltpu.make_async_remote_copy(
        halo_out.at[1], halo_d.at[1], halo_send.at[1], halo_recv.at[1],
        device_id=(left, me), device_id_type=MESH)
    to_right.start()
    to_left.start()

    for side, start in ((0, 8), (1, 12)):
        bits, places, taken = ranks(named(g, start))
        for s in range(BLK_DEV):
            row_map[2 * side * BLK_DEV + s] = side * (HALO + BLK_DEV) + jnp.minimum(places[s], HALO - 1)
    for s in range(BLK_DEV):
        row_map[BLK_DEV + s] = HALO + s

    def own_row_twice(s, carry):
        for q in range(KNZ // 2):
            keep_both(ext2, HALO + s, q, own[s, :, q * 128 : (q + 1) * 128])
        return carry

    lax.fori_loop(0, BLK_DEV, own_row_twice, 0)

    def batch_table(b):
        ids = [act[e, g * ROWS + b] for e in range(ACT)]
        blocks = [jnp.int32(0), jnp.int32(0)]
        count = jnp.int32(0)
        for e in range(ACT):
            mine = ((ids[e] >> 3) & (ROWS - 1)) == me
            blocks[0] = jnp.where(mine & (count == 0), ids[e], blocks[0])
            blocks[1] = jnp.where(mine & (count == 1), ids[e], blocks[1])
            count = count + mine.astype(jnp.int32)
        packed = [jnp.int32(0)] * KNZ
        running = jnp.int32(0)
        for c in range(2):
            group = jnp.minimum(((blocks[c] >> 7) - g + 1) & 15, 2)
            tab_row[2 * b + c] = row_map[group * BLK_DEV + (blocks[c] & 7)]
            valid = count > c
            for m in range(KNZ):
                column = pat[m, blocks[c]]
                gap = column ^ ids[0]
                for e in range(1, ACT):
                    gap = jnp.minimum(gap, column ^ ids[e])
                match = (gap == 0) & valid
                for p in range(m + 1 if c == 0 else KNZ):
                    packed[p] = jnp.where(match & (running == p), c * KNZ + m, packed[p])
                tab_pos[b * 16 + c * KNZ + m] = jnp.where(match, jnp.minimum(running, KNZ - 1), KNZ)
                running = running + match.astype(jnp.int32)
        for p in range(KNZ):
            tab_src[b * KNZ + p] = packed[p]
        tab_row[2 * ROWS + b] = count

    masks = half_masks()

    def pack_rows(b, target):
        for q in range(KNZ // 2):
            a = tab_src[b * KNZ + 2 * q]
            c = tab_src[b * KNZ + 2 * q + 1]
            target[b if target is send_d else me, q] = two_blocks(
                ext2, tab_row[2 * b + (a >> 3)], a & 7, tab_row[2 * b + (c >> 3)], c & 7, masks)

    def first_copy(i):
        p = peer(i)
        return pltpu.make_async_remote_copy(
            send_d.at[p], recv_d.at[me], a2a_send.at[i], a2a_recv.at[i],
            device_id=(g, p), device_id_type=MESH)

    batch_table(peer(0))
    to_right.wait_recv()
    to_left.wait_recv()
    for side in range(2):
        for i in range(HALO):
            for q in range(KNZ // 2):
                keep_both(ext2, side * (HALO + BLK_DEV) + i, q, halo_d[side, i, :, q * 128 : (q + 1) * 128])

    def send_first(i, carry):
        pack_rows(peer(i), send_d)
        first_copy(i).start()
        following = peer(i + 1)
        batch_table(following)
        return carry

    lax.fori_loop(0, ROWS - 1, send_first, 0)
    pack_rows(me, recv_d)

    def match_row(k, carry):
        block = act[k, g * ROWS + me]
        tab_owner[k] = (block >> 3) & (ROWS - 1)
        local = [jnp.int32(KNZ)] * ACT
        running = jnp.int32(0)
        for m in range(KNZ):
            column = pat[m, block]
            found = jnp.int32(ACT)
            for j in range(ACT):
                same = column == act[j, g * ROWS + me]
                found = jnp.where(same, j, found)
                local[j] = jnp.where(same, running, local[j])
            tab_j[k * KNZ + m] = found
            tab_rank[k * KNZ + m] = jnp.where(found < ACT, running, 64)
            running = running + (found < ACT).astype(jnp.int32)
        for j in range(ACT):
            tab_local[k * ACT + j] = local[j]
        tab_q[k] = running
        return carry

    lax.fori_loop(0, ACT, match_row, 0)

    def start_row(k, most):
        start = jnp.int32(0)
        for j in range(ACT):
            start = start + jnp.where((j < k) & (tab_owner[j] == tab_owner[k]), tab_q[j], 0)
        tab_start[k] = start
        for j in range(ACT):
            local = tab_local[k * ACT + j]
            tab_dpos[k * ACT + j] = jnp.where(local < KNZ, jnp.minimum(start + local, KNZ - 1), KNZ)
        return jnp.maximum(most, start + tab_q[k])

    most = lax.fori_loop(0, ACT, start_row, jnp.int32(0))
    overflow = jnp.maximum(overflow, (most > KNZ).astype(jnp.int32))

    row_flags[me] = jnp.full((8, 128), overflow, jnp.int32)

    def row_flag_copy(i):
        p = peer(i)
        return pltpu.make_async_remote_copy(
            row_flags.at[me], row_flags.at[me], flag_send.at[i], flag_recv.at[i],
            device_id=(g, p), device_id_type=MESH)

    def region_flag_copy(r):
        return pltpu.make_async_remote_copy(
            region_flags.at[0, r], region_flags.at[1, r], flag_send.at[15 + r], flag_recv.at[15 + r],
            device_id=(lax.rem(g + 2**r, 16), me), device_id_type=MESH)

    def merge_flags(r):
        region_flag_copy(r).wait_recv()
        merged = jnp.maximum(region_flags[0, r], region_flags[1, r])
        if r < 3:
            region_flags[0, r + 1] = merged
            region_flag_copy(r + 1).start()
        else:
            flag_out[...] = merged

    def send_flag(i, carry):
        row_flag_copy(i).start()
        return carry

    lax.fori_loop(0, ROWS - 1, send_flag, 0)

    def slot_table(r, carry):
        entries = [jnp.int32(0), jnp.int32(0)]
        count = jnp.int32(0)
        for k in range(ACT):
            mine = tab_owner[k] == r
            entries[0] = jnp.where(mine & (count == 0), k, entries[0])
            entries[1] = jnp.where(mine & (count == 1), k, entries[1])
            count = count + mine.astype(jnp.int32)
        packed = [jnp.int32(0)] * KNZ
        for c in range(2):
            k = entries[c]
            start = jnp.where(count > c, tab_start[k], 64)
            for m in range(KNZ):
                place = start + tab_rank[k * KNZ + m]
                code = k * ACT + jnp.minimum(tab_j[k * KNZ + m], ACT - 1)
                for p in range(m + 1 if c == 0 else KNZ):
                    packed[p] = jnp.where(place == p, code, packed[p])
        for p in range(KNZ):
            tab_h[r * KNZ + p] = packed[p]
        return carry

    lax.fori_loop(0, ROWS, slot_table, 0)

    rows2[:, :, KNZ // 2] = jnp.zeros((2, ROWS, BS, 128), BF16)
    hvar[:, :, KNZ // 2] = jnp.zeros((2, ROWS, BS, 128), BF16)
    expanded[2 * ROWS] = jnp.zeros((KNZ // 2, BS, 128), BF16)
    for side in range(2):
        halo_in[side, HALO] = jnp.zeros((BS, WIDTH), BF16)

    x_copy.wait()

    def transpose_chunk(i, carry):
        points = pl.ds(pl.multiple_of(i * 128, 128), 128)
        xt[:, points] = jnp.transpose(xv[points, :])
        return carry

    lax.fori_loop(0, PTS // 128, transpose_chunk, 0)

    def spread_slot(r):
        for q in range(KNZ // 2):
            keep_both(rows2, r, q, recv_d[r, q])

    spread_slot(me)

    def take_first(i, carry):
        first_copy(i).wait_recv()
        spread_slot(sender(i))
        return carry

    lax.fori_loop(0, ROWS - 1, take_first, 0)

    def assemble_row(k, carry):
        owner = tab_owner[k]
        for q in range(ACT // 2):
            dfull[pl.ds(pl.multiple_of(k * BS, BS), BS), q * 128 : (q + 1) * 128] = pair_of_blocks(
                rows2, owner, tab_dpos[k * ACT + 2 * q], tab_dpos[k * ACT + 2 * q + 1], masks)
        return carry

    lax.fori_loop(0, ACT, assemble_row, 0)

    def density_chunk(i, carry):
        points = pl.ds(pl.multiple_of(i * CHUNK, CHUNK), CHUNK)
        x = xv[points, :]
        part = jnp.zeros((CHUNK, 128), F32)
        for n in range(COLS // CHUNK):
            product = jnp.dot(x, dfull[:, n * CHUNK : (n + 1) * CHUNK], preferred_element_type=F32)
            product = product * x[:, n * CHUNK : (n + 1) * CHUNK].astype(F32)
            part = part + (product[:, :128] + product[:, 128:])
        dens = jnp.sum(jnp.transpose(part), axis=0, keepdims=True)
        dens_out[:, points] = dens
        svec[:, points] = weights[:, points] * jnp.tanh(dens)
        return carry

    lax.fori_loop(0, PTS // CHUNK, density_chunk, 0)

    def take_flag(i, carry):
        row_flag_copy(i).wait_recv()
        return carry

    lax.fori_loop(0, ROWS - 1, take_flag, 0)
    merged = row_flags[0]
    for r in range(1, ROWS):
        merged = jnp.maximum(merged, row_flags[r])
    region_flags[0, 0] = merged
    region_flag_copy(0).start()

    def ham_chunk(i, carry):
        scaled = (xt[pl.ds(pl.multiple_of(i * CHUNK, CHUNK), CHUNK), :].astype(F32) * svec[...]).astype(BF16)
        for n in range(COLS // CHUNK):
            block = jnp.dot(scaled, xv[:, n * CHUNK : (n + 1) * CHUNK], preferred_element_type=F32)
            for half in range(CHUNK // 128):
                part = block[:, half * 128 : (half + 1) * 128]
                swapped = swap_halves(part).astype(BF16)
                part = part.astype(BF16)
                for kk in range(CHUNK // BS):
                    entry = i * (CHUNK // BS) + kk
                    hrows[0, entry, 2 * n + half] = part[kk * BS : (kk + 1) * BS]
                    hrows[1, entry, 2 * n + half] = swapped[kk * BS : (kk + 1) * BS]
        return carry

    lax.fori_loop(0, COLS // CHUNK, ham_chunk, 0)

    def pack_slot(r, target, target_row):
        for q in range(KNZ // 2):
            a = tab_h[r * KNZ + 2 * q]
            b = tab_h[r * KNZ + 2 * q + 1]
            target[target_row, q] = two_blocks(hrows, a >> 4, a & 15, b >> 4, b & 15, masks)

    def second_copy(i):
        p = peer(i)
        return pltpu.make_async_remote_copy(
            send_h.at[p], recv_h.at[me], a2a_send.at[15 + i], a2a_recv.at[15 + i],
            device_id=(g, p), device_id_type=MESH)

    def send_second(i, carry):
        p = peer(i)
        pack_slot(p, send_h, p)
        second_copy(i).start()
        return carry

    lax.fori_loop(0, ROWS - 1, send_second, 0)
    pack_slot(me, recv_h, me)

    merge_flags(0)
    merge_flags(1)
    merge_flags(2)

    def expand_slot(b):
        for q in range(KNZ // 2):
            keep_both(hvar, b, q, recv_h[b, q])
        for c in range(2):
            for q in range(KNZ // 2):
                expanded[2 * b + c, q] = pair_of_blocks(
                    hvar, b, tab_pos[b * 16 + c * KNZ + 2 * q], tab_pos[b * 16 + c * KNZ + 2 * q + 1], masks)

    expand_slot(me)

    def take_second(i, carry):
        second_copy(i).wait_recv()
        expand_slot(sender(i))
        return carry

    lax.fori_loop(0, ROWS - 1, take_second, 0)

    def sum_row(t):
        picks = []
        for b in range(ROWS):
            count = tab_row[2 * ROWS + b]
            picks.append(jnp.where(
                (tab_row[2 * b] == t) & (count > 0), 2 * b,
                jnp.where((tab_row[2 * b + 1] == t) & (count > 1), 2 * b + 1, 2 * ROWS)))
        total = expanded[picks[0]].astype(F32)
        for b in range(1, ROWS):
            total = total + expanded[picks[b]].astype(F32)
        return total

    to_right.wait_send()
    to_left.wait_send()

    def side_row(t, carry):
        for side in range(2):
            total = sum_row(side * (HALO + BLK_DEV) + t).astype(BF16)
            for q in range(KNZ // 2):
                halo_out[side, t, :, q * 128 : (q + 1) * 128] = total[q]
        return carry

    lax.fori_loop(0, HALO, side_row, 0)

    back_left = pltpu.make_async_remote_copy(
        halo_out.at[0], halo_in.at[0, pl.ds(0, HALO)], halo_send.at[2], halo_recv.at[2],
        device_id=(left, me), device_id_type=MESH)
    back_right = pltpu.make_async_remote_copy(
        halo_out.at[1], halo_in.at[1, pl.ds(0, HALO)], halo_send.at[3], halo_recv.at[3],
        device_id=(right, me), device_id_type=MESH)
    back_left.start()
    back_right.start()

    def own_row(t, carry):
        total = sum_row(HALO + t)
        for q in range(KNZ // 2):
            ham_out[t, :, q * 128 : (q + 1) * 128] = total[q]
        return carry

    lax.fori_loop(0, BLK_DEV, own_row, 0)
    merge_flags(3)
    back_left.wait_recv()
    back_right.wait_recv()

    def add_row(t, carry):
        ham_out[t] = (
            ham_out[t]
            + halo_in[0, back_map[t]].astype(F32)
            + halo_in[1, back_map[BLK_DEV + t]].astype(F32)
        )
        return carry

    lax.fori_loop(0, BLK_DEV, add_row, 0)

    def finish(i, carry):
        first_copy(i).wait_send()
        second_copy(i).wait_send()
        row_flag_copy(i).wait_send()
        return carry

    lax.fori_loop(0, ROWS - 1, finish, 0)
    for r in range(4):
        region_flag_copy(r).wait_send()
    back_left.wait_send()
    back_right.wait_send()


def specs():
    vmem = pl.BlockSpec(memory_space=pltpu.VMEM)
    smem = pl.BlockSpec(memory_space=pltpu.SMEM)
    hbm = pl.BlockSpec(memory_space=pl.ANY)
    return [smem, smem, vmem, hbm, hbm], vmem


def full_capacity(act, pat, weights, x, d):
    in_specs, vmem = specs()
    return pl.pallas_call(
        full_kernel,
        out_shape=(
            jax.ShapeDtypeStruct((1, PTS), F32),
            jax.ShapeDtypeStruct((BLK_DEV, BS, WIDTH), F32),
        ),
        in_specs=in_specs,
        out_specs=(vmem, vmem),
        scratch_shapes=[
            pltpu.VMEM((PTS, COLS), BF16),
            pltpu.VMEM((COLS, PTS), BF16),
            pltpu.VMEM((3 * BLK_DEV, BS, WIDTH), BF16),
            pltpu.VMEM((ROWS, 2, BS, WIDTH), BF16),
            pltpu.VMEM((2 * ROWS, BS, WIDTH), BF16),
            pltpu.VMEM((2, ACT, KNZ // 2 + 1, BS, 128), BF16),
            pltpu.VMEM((COLS, COLS), BF16),
            pltpu.VMEM((1, PTS), F32),
            pltpu.VMEM((2, ACT, ACT // 2 + 1, BS, 128), BF16),
            pltpu.VMEM((ROWS, 2, BS, WIDTH), BF16),
            pltpu.VMEM((ROWS, 3, BS, WIDTH), BF16),
            pltpu.VMEM((2, BLK_DEV, BS, WIDTH), BF16),
            pltpu.VMEM((2, BLK_DEV, BS, WIDTH), BF16),
            pltpu.SMEM((3 * ROWS,), jnp.int32),
            pltpu.SMEM((ACT,), jnp.int32),
            pltpu.SMEM((ACT * ACT,), jnp.int32),
            pltpu.SMEM((ACT * KNZ,), jnp.int32),
            pltpu.SMEM((2 * ROWS,), jnp.int32),
            pltpu.SemaphoreType.DMA((2,)),
            pltpu.SemaphoreType.DMA((4,)),
            pltpu.SemaphoreType.DMA((4,)),
            pltpu.SemaphoreType.DMA((30,)),
            pltpu.SemaphoreType.DMA((30,)),
        ],
        compiler_params=pltpu.CompilerParams(
            collective_id=1, has_side_effects=True, vmem_limit_bytes=56 << 20
        ),
    )(act, pat, weights, x, d)


def packed_capacity(act, pat, weights, x, d):
    in_specs, vmem = specs()
    half = KNZ // 2
    return pl.pallas_call(
        packed_kernel,
        out_shape=(
            jax.ShapeDtypeStruct((1, PTS), F32),
            jax.ShapeDtypeStruct((BLK_DEV, BS, WIDTH), F32),
            jax.ShapeDtypeStruct((8, 128), jnp.int32),
        ),
        in_specs=in_specs,
        out_specs=(vmem, vmem, vmem),
        scratch_shapes=[
            pltpu.VMEM((PTS, COLS), BF16),
            pltpu.VMEM((COLS, PTS), BF16),
            pltpu.VMEM((BLK_DEV, BS, WIDTH), BF16),
            pltpu.VMEM((2, HALO, BS, WIDTH), BF16),
            pltpu.VMEM((2, BLK_DEV + 2 * HALO, half, BS, 128), BF16),
            pltpu.VMEM((ROWS, half, BS, 128), BF16),
            pltpu.VMEM((ROWS, half, BS, 128), BF16),
            pltpu.VMEM((2, ROWS, half + 1, BS, 128), BF16),
            pltpu.VMEM((COLS, COLS), BF16),
            pltpu.VMEM((1, PTS), F32),
            pltpu.VMEM((2, ACT, ACT // 2, BS, 128), BF16),
            pltpu.VMEM((ROWS, half, BS, 128), BF16),
            pltpu.VMEM((ROWS, half, BS, 128), BF16),
            pltpu.VMEM((2, ROWS, half + 1, BS, 128), BF16),
            pltpu.VMEM((2 * ROWS + 1, half, BS, 128), BF16),
            pltpu.VMEM((2, HALO, BS, WIDTH), BF16),
            pltpu.VMEM((2, HALO + 1, BS, WIDTH), BF16),
            pltpu.VMEM((ROWS, 8, 128), jnp.int32),
            pltpu.VMEM((2, 4, 8, 128), jnp.int32),
            pltpu.SMEM((2 * HALO,), jnp.int32),
            pltpu.SMEM((3 * BLK_DEV,), jnp.int32),
            pltpu.SMEM((2 * BLK_DEV,), jnp.int32),
            pltpu.SMEM((3 * ROWS,), jnp.int32),
            pltpu.SMEM((ROWS * KNZ,), jnp.int32),
            pltpu.SMEM((ROWS * 2 * KNZ,), jnp.int32),
            pltpu.SMEM((ACT * KNZ,), jnp.int32),
            pltpu.SMEM((ACT * KNZ,), jnp.int32),
            pltpu.SMEM((ACT * ACT,), jnp.int32),
            pltpu.SMEM((ACT,), jnp.int32),
            pltpu.SMEM((ACT,), jnp.int32),
            pltpu.SMEM((ACT,), jnp.int32),
            pltpu.SMEM((ACT * ACT,), jnp.int32),
            pltpu.SMEM((ROWS * KNZ,), jnp.int32),
            pltpu.SemaphoreType.DMA((2,)),
            pltpu.SemaphoreType.DMA((4,)),
            pltpu.SemaphoreType.DMA((4,)),
            pltpu.SemaphoreType.DMA((30,)),
            pltpu.SemaphoreType.DMA((30,)),
            pltpu.SemaphoreType.DMA((19,)),
            pltpu.SemaphoreType.DMA((19,)),
        ],
        compiler_params=pltpu.CompilerParams(
            collective_id=0, has_side_effects=True, vmem_limit_bytes=56 << 20
        ),
    )(act, pat, weights, x, d)


def shards(basis_values, grid_weights, density_blocks, pattern, active):
    args = (
        active.T,
        pattern.T,
        grid_weights.reshape(1, PTS),
        basis_values,
        density_blocks.reshape(BLK_DEV, BS, WIDTH),
    )
    dens, ham, flag = packed_capacity(*args)
    dens, ham = lax.cond(flag[0, 0] > 0, lambda: tuple(full_capacity(*args)), lambda: (dens, ham))
    return dens.reshape(PTS), ham.reshape(BLK_DEV * BS, WIDTH)


def solution(mesh):
    placed = (
        P(("region", "rows"), None),
        P(("region", "rows")),
        P(("region", "rows"), None),
        P(),
        P(),
    )
    return jax.shard_map(
        shards,
        mesh=mesh,
        in_specs=placed,
        out_specs=(P(("region", "rows")), P(("region", "rows"), None)),
        check_vma=False,
    )
```

```python
import functools

import jax
import jax.numpy as jnp
from jax import lax
from jax.experimental import pallas as pl
from jax.experimental.pallas import tpu as pltpu
from jax.sharding import PartitionSpec as P

BS = 64
BLK_DEV = 8
KNZ = 8
ACT = 16
PTS = 1536
ROWS = 16
WIDTH = KNZ * BS
COLS = ACT * BS
CHUNK = 256
HALO = 1
MESH = pl.DeviceIdType.MESH
F32 = jnp.float32
BF16 = jnp.bfloat16
PEERS = tuple(
    (dy, dz)
    for dz in (4, 3, 5, 2, 6, 1, 7, 0)
    for dy in (0, 1)
    if (dy, dz) != (0, 0)
)


def half_masks():
    lane = lax.broadcasted_iota(jnp.int32, (BS, 128), 1)
    low = jnp.where(lane < BS, 1.0, 0.0).astype(BF16)
    high = jnp.where(lane < BS, 0.0, 1.0).astype(BF16)
    return low, high


def two_blocks(source, row_a, block_a, row_b, block_b, masks):
    low, high = masks
    a = source[block_a & 1, row_a, block_a >> 1]
    b = source[1 - (block_b & 1), row_b, block_b >> 1]
    return a * low + b * high


def pair_of_blocks(source, row, first, second, masks):
    return two_blocks(source, row, first, row, second, masks)


def swap_halves(values):
    return pltpu.roll(values, 64, 1)


def keep_both(target, row, part, values):
    target[0, row, part] = values
    target[1, row, part] = swap_halves(values.astype(F32)).astype(BF16)


def full_kernel(
    act, pat, weights, x_hbm, d_hbm,
    dens_out, ham_out,
    xv, xt, ext, send_d, recv_d, rows2, dfull, svec, hrows, send_h, recv_h,
    halo_out, halo_in,
    tab_row, tab_arr, tab_m, tab_j, tab_slot,
    local_sems, halo_send, halo_recv, a2a_send, a2a_recv,
):
    g = lax.axis_index("region")
    me = lax.axis_index("rows")
    y = lax.div(me, 8)
    z = lax.rem(me, 8)
    left, right = lax.rem(g + 15, 16), lax.rem(g + 1, 16)

    def peer(dy, dz):
        return lax.rem(y + dy, 2) * 8 + lax.rem(z + dz, 8)

    x_copy = pltpu.make_async_copy(x_hbm, xv, local_sems.at[0])
    x_copy.start()
    d_copy = pltpu.make_async_copy(d_hbm, ext.at[pl.ds(BLK_DEV, BLK_DEV)], local_sems.at[1])
    d_copy.start()

    barrier = pltpu.get_barrier_semaphore()
    for n in (left, right):
        pl.semaphore_signal(barrier, inc=1, device_id=(n, me), device_id_type=MESH)
    for dy, dz in PEERS:
        pl.semaphore_signal(barrier, inc=1, device_id=(g, peer(dy, dz)), device_id_type=MESH)
    pl.semaphore_wait(barrier, 17)

    to_right = pltpu.make_async_remote_copy(
        d_hbm, ext.at[pl.ds(0, BLK_DEV)], halo_send.at[0], halo_recv.at[0],
        device_id=(right, me), device_id_type=MESH)
    to_left = pltpu.make_async_remote_copy(
        d_hbm, ext.at[pl.ds(2 * BLK_DEV, BLK_DEV)], halo_send.at[1], halo_recv.at[1],
        device_id=(left, me), device_id_type=MESH)
    to_right.start()
    to_left.start()

    def rows_of_batch(b, carry):
        first = jnp.int32(0)
        second = jnp.int32(0)
        count = jnp.int32(0)
        for e in range(ACT):
            block = act[e, g * ROWS + b]
            mine = ((block >> 3) & (ROWS - 1)) == me
            row = jnp.minimum(((block >> 7) - g + 1) & 15, 2) * BLK_DEV + (block & 7)
            first = jnp.where(mine & (count == 0), row, first)
            second = jnp.where(mine & (count == 1), row, second)
            count = count + mine.astype(jnp.int32)
        tab_row[2 * b] = first
        tab_row[2 * b + 1] = second
        tab_row[2 * ROWS + b] = count
        return carry

    lax.fori_loop(0, ROWS, rows_of_batch, 0)

    d_copy.wait()
    to_right.wait_recv()
    to_left.wait_recv()

    first_copies = []
    for i, (dy, dz) in enumerate(PEERS):
        p = peer(dy, dz)
        for c in range(2):
            send_d[p, c] = ext[tab_row[2 * p + c]]
        copy = pltpu.make_async_remote_copy(
            send_d.at[p], recv_d.at[pl.ds(2 * me, 2)], a2a_send.at[i], a2a_recv.at[i],
            device_id=(g, p), device_id_type=MESH)
        copy.start()
        first_copies.append(copy)
    for c in range(2):
        recv_d[2 * me + c] = ext[tab_row[2 * me + c]]

    ids = [act[k, g * ROWS + me] for k in range(ACT)]
    owners = [(i >> 3) & (ROWS - 1) for i in ids]
    for k in range(ACT):
        earlier = jnp.int32(0)
        for j in range(k):
            earlier = earlier + (owners[j] == owners[k]).astype(jnp.int32)
        tab_arr[k] = owners[k] * 2 + jnp.minimum(earlier, 1)

    def slot_entries(s, carry):
        entry = jnp.int32(0)
        for k in range(ACT):
            entry = jnp.where(tab_arr[k] == s, k, entry)
        tab_slot[s] = entry
        return carry

    lax.fori_loop(0, 2 * ROWS, slot_entries, 0)

    def match_row(k, carry):
        block = act[k, g * ROWS + me]
        found_m = [jnp.int32(KNZ)] * ACT
        for m in range(KNZ):
            column = pat[m, block]
            found = jnp.int32(ACT)
            for j in range(ACT):
                same = column == act[j, g * ROWS + me]
                found = jnp.where(same, j, found)
                found_m[j] = jnp.where(same, m, found_m[j])
            tab_j[k * KNZ + m] = found
        for j in range(ACT):
            tab_m[k * ACT + j] = found_m[j]
        return carry

    lax.fori_loop(0, ACT, match_row, 0)

    rows2[:, :, KNZ // 2] = jnp.zeros((2, ACT, BS, 128), BF16)
    hrows[:, :, ACT // 2] = jnp.zeros((2, ACT, BS, 128), BF16)
    recv_h[:, 2] = jnp.zeros((ROWS, BS, WIDTH), BF16)

    x_copy.wait()

    def transpose_chunk(i, carry):
        points = pl.ds(pl.multiple_of(i * 128, 128), 128)
        xt[:, points] = jnp.transpose(xv[points, :])
        return carry

    lax.fori_loop(0, PTS // 128, transpose_chunk, 0)

    masks = half_masks()
    for copy in first_copies:
        copy.wait_recv()

    def spread_row(k, carry):
        row = recv_d[tab_arr[k]]
        for q in range(KNZ // 2):
            part = row[:, q * 128 : (q + 1) * 128]
            rows2[0, k, q] = part
            rows2[1, k, q] = swap_halves(part.astype(F32)).astype(BF16)
        for q in range(ACT // 2):
            first = tab_m[k * ACT + 2 * q]
            second = tab_m[k * ACT + 2 * q + 1]
            dfull[pl.ds(pl.multiple_of(k * BS, BS), BS), q * 128 : (q + 1) * 128] = pair_of_blocks(
                rows2, k, first, second, masks)
        return carry

    lax.fori_loop(0, ACT, spread_row, 0)

    def density_chunk(i, carry):
        points = pl.ds(pl.multiple_of(i * CHUNK, CHUNK), CHUNK)
        x = xv[points, :]
        part = jnp.zeros((CHUNK, 128), F32)
        for n in range(COLS // CHUNK):
            product = jnp.dot(x, dfull[:, n * CHUNK : (n + 1) * CHUNK], preferred_element_type=F32)
            product = product * x[:, n * CHUNK : (n + 1) * CHUNK].astype(F32)
            part = part + (product[:, :128] + product[:, 128:])
        dens = jnp.sum(jnp.transpose(part), axis=0, keepdims=True)
        for half in range(CHUNK // 128):
            row = pl.ds(i * (CHUNK // 128) + half, 1)
            dens_half = dens[:, half * 128 : (half + 1) * 128]
            dens_out[row, :] = dens_half
            svec[:, pl.ds(pl.multiple_of(i * CHUNK + half * 128, 128), 128)] = weights[row, :] * jnp.tanh(dens_half)
        return carry

    lax.fori_loop(0, PTS // CHUNK, density_chunk, 0)

    def ham_chunk(i, carry):
        scaled = (xt[pl.ds(pl.multiple_of(i * CHUNK, CHUNK), CHUNK), :].astype(F32) * svec[...]).astype(BF16)
        for n in range(COLS // CHUNK):
            block = jnp.dot(scaled, xv[:, n * CHUNK : (n + 1) * CHUNK], preferred_element_type=F32)
            for half in range(CHUNK // 128):
                part = block[:, half * 128 : (half + 1) * 128]
                swapped = swap_halves(part).astype(BF16)
                part = part.astype(BF16)
                for kk in range(CHUNK // BS):
                    entry = i * (CHUNK // BS) + kk
                    hrows[0, entry, 2 * n + half] = part[kk * BS : (kk + 1) * BS]
                    hrows[1, entry, 2 * n + half] = swapped[kk * BS : (kk + 1) * BS]
        return carry

    lax.fori_loop(0, COLS // CHUNK, ham_chunk, 0)

    for copy in first_copies:
        copy.wait_send()

    def gather_slots(p, target, target_row):
        for c in range(2):
            k = tab_slot[2 * p + c]
            for q in range(KNZ // 2):
                first = tab_j[k * KNZ + 2 * q]
                second = tab_j[k * KNZ + 2 * q + 1]
                target[target_row, c, :, q * 128 : (q + 1) * 128] = pair_of_blocks(
                    hrows, k, first, second, masks)

    second_copies = []
    for i, (dy, dz) in enumerate(PEERS):
        p = peer(dy, dz)
        gather_slots(p, send_h, p)
        copy = pltpu.make_async_remote_copy(
            send_h.at[p], recv_h.at[me, pl.ds(0, 2)], a2a_send.at[15 + i], a2a_recv.at[15 + i],
            device_id=(g, p), device_id_type=MESH)
        copy.start()
        second_copies.append(copy)
    gather_slots(me, recv_h, me)
    for copy in second_copies:
        copy.wait_recv()

    def sum_row(t):
        picks = []
        for b in range(ROWS):
            count = tab_row[2 * ROWS + b]
            picks.append(jnp.where(
                (tab_row[2 * b] == t) & (count > 0), 0,
                jnp.where((tab_row[2 * b + 1] == t) & (count > 1), 1, 2)))
        total = recv_h[0, picks[0]].astype(F32)
        for b in range(1, ROWS):
            total = total + recv_h[b, picks[b]].astype(F32)
        return total

    def side_row(t, carry):
        for side, base in ((0, 0), (1, 2 * BLK_DEV)):
            halo_out[side, t] = sum_row(base + t).astype(BF16)
        return carry

    lax.fori_loop(0, BLK_DEV, side_row, 0)

    back_left = pltpu.make_async_remote_copy(
        halo_out.at[0], halo_in.at[0], halo_send.at[2], halo_recv.at[2],
        device_id=(left, me), device_id_type=MESH)
    back_right = pltpu.make_async_remote_copy(
        halo_out.at[1], halo_in.at[1], halo_send.at[3], halo_recv.at[3],
        device_id=(right, me), device_id_type=MESH)
    back_left.start()
    back_right.start()

    def own_row(t, carry):
        ham_out[t] = sum_row(BLK_DEV + t)
        return carry

    lax.fori_loop(0, BLK_DEV, own_row, 0)
    back_left.wait_recv()
    back_right.wait_recv()

    def add_row(t, carry):
        ham_out[t] = ham_out[t] + halo_in[0, t].astype(F32) + halo_in[1, t].astype(F32)
        return carry

    lax.fori_loop(0, BLK_DEV, add_row, 0)

    for copy in second_copies:
        copy.wait_send()
    for copy in (to_right, to_left, back_left, back_right):
        copy.wait_send()


def offset_of(i):
    j = lax.div(i, 2)
    dz = 4 + lax.div(j + 1, 2) * (1 - 2 * lax.rem(j, 2))
    return 1 - lax.rem(i, 2), dz


def packed_kernel(
    act, pat, weights, x_hbm, d_hbm,
    dens_out, ham_out, flag_out,
    xv, xt, own, halo_d, ext2, send_d, recv_d, rows2, dfull, svec, hrows, send_h,
    recv_h, hvar, expanded, halo_out, halo_in, row_flags, region_flags,
    halo_src, row_map, back_map, tab_row, tab_src, tab_pos,
    tab_j, tab_rank, tab_local, tab_q, tab_start, tab_owner, tab_dpos, tab_h, tab_turn, tab_place, tab_order,
    local_sems, halo_send, halo_recv, a2a_send, a2a_recv, flag_send, flag_recv,
):
    g = lax.axis_index("region")
    me = lax.axis_index("rows")
    y = lax.div(me, 8)
    z = lax.rem(me, 8)
    left, right = lax.rem(g + 15, 16), lax.rem(g + 1, 16)

    def peer(i):
        dy, dz = offset_of(i)
        return lax.rem(y + dy, 2) * 8 + lax.rem(z + dz, 8)

    def sender(i):
        dy, dz = offset_of(i)
        return lax.rem(y + dy, 2) * 8 + lax.rem(z + 8 - dz, 8)

    x_copy = pltpu.make_async_copy(x_hbm, xv, local_sems.at[0])
    d_copy = pltpu.make_async_copy(d_hbm, own, local_sems.at[1])
    d_copy.start()
    x_copy.start()

    barrier = pltpu.get_barrier_semaphore()
    for n in (left, right) + tuple(lax.rem(g + 16 - hop, 16) for hop in (2, 4, 8)):
        pl.semaphore_signal(barrier, inc=1, device_id=(n, me), device_id_type=MESH)

    def greet(i, carry):
        pl.semaphore_signal(barrier, inc=1, device_id=(g, peer(i)), device_id_type=MESH)
        return carry

    lax.fori_loop(0, ROWS - 1, greet, 0)

    def named(region, start):
        def one(b, mask):
            for e in range(start, start + 4):
                block = act[e, region * ROWS + b]
                bit = (1 + (block & 1)) * (1 + 3 * ((block >> 1) & 1)) * (1 + 15 * ((block >> 2) & 1))
                mask = mask | jnp.where(((block >> 3) & (ROWS - 1)) == me, bit, 0)
            return mask

        return lax.fori_loop(0, ROWS, one, jnp.int32(0))

    def ranks(mask):
        taken = jnp.int32(0)
        bits, places = [], []
        for s in range(BLK_DEV):
            bit = (mask >> s) & 1
            bits.append(bit)
            places.append(taken)
            taken = taken + bit
        return bits, places, taken

    overflow = jnp.int32(0)
    for side, mask in enumerate((named(right, 8), named(left, 12))):
        bits, places, taken = ranks(mask)
        for i in range(HALO):
            source = jnp.int32(0)
            for s in range(BLK_DEV):
                source = jnp.where((bits[s] == 1) & (places[s] == i), s, source)
            halo_src[side * HALO + i] = source
        for s in range(BLK_DEV):
            back_map[side * BLK_DEV + s] = jnp.where(bits[s] == 1, jnp.minimum(places[s], HALO - 1), HALO)
        overflow = jnp.maximum(overflow, (taken > HALO).astype(jnp.int32))

    d_copy.wait()
    for side in range(2):
        for i in range(HALO):
            halo_out[side, i] = own[halo_src[side * HALO + i]]
    pl.semaphore_wait(barrier, 20)

    to_right = pltpu.make_async_remote_copy(
        halo_out.at[0], halo_d.at[0], halo_send.at[0], halo_recv.at[0],
        device_id=(right, me), device_id_type=MESH)
    to_left = pltpu.make_async_remote_copy(
        halo_out.at[1], halo_d.at[1], halo_send.at[1], halo_recv.at[1],
        device_id=(left, me), device_id_type=MESH)
    to_right.start()
    to_left.start()

    for side, start in ((0, 8), (1, 12)):
        bits, places, taken = ranks(named(g, start))
        for s in range(BLK_DEV):
            row_map[2 * side * BLK_DEV + s] = side * (HALO + BLK_DEV) + jnp.minimum(places[s], HALO - 1)
    for s in range(BLK_DEV):
        row_map[BLK_DEV + s] = HALO + s

    def own_row_twice(s, carry):
        for q in range(KNZ // 2):
            keep_both(ext2, HALO + s, q, own[s, :, q * 128 : (q + 1) * 128])
        return carry

    lax.fori_loop(0, BLK_DEV, own_row_twice, 0)

    def batch_table(b):
        ids = [act[e, g * ROWS + b] for e in range(ACT)]
        blocks = [jnp.int32(0), jnp.int32(0)]
        count = jnp.int32(0)
        for e in range(ACT):
            mine = ((ids[e] >> 3) & (ROWS - 1)) == me
            blocks[0] = jnp.where(mine & (count == 0), ids[e], blocks[0])
            blocks[1] = jnp.where(mine & (count == 1), ids[e], blocks[1])
            count = count + mine.astype(jnp.int32)
        packed = [jnp.int32(0)] * KNZ
        running = jnp.int32(0)
        for c in range(2):
            group = jnp.minimum(((blocks[c] >> 7) - g + 1) & 15, 2)
            tab_row[2 * b + c] = row_map[group * BLK_DEV + (blocks[c] & 7)]
            valid = count > c
            for m in range(KNZ):
                column = pat[m, blocks[c]]
                gap = column ^ ids[0]
                for e in range(1, ACT):
                    gap = jnp.minimum(gap, column ^ ids[e])
                match = (gap == 0) & valid
                for p in range(m + 1 if c == 0 else KNZ):
                    packed[p] = jnp.where(match & (running == p), c * KNZ + m, packed[p])
                tab_pos[b * 16 + c * KNZ + m] = jnp.where(match, jnp.minimum(running, KNZ - 1), KNZ)
                running = running + match.astype(jnp.int32)
        for p in range(KNZ):
            tab_src[b * KNZ + p] = packed[p]
        tab_row[2 * ROWS + b] = count

    masks = half_masks()

    def pack_rows(b, target):
        for q in range(KNZ // 2):
            a = tab_src[b * KNZ + 2 * q]
            c = tab_src[b * KNZ + 2 * q + 1]
            target[b if target is send_d else me, q] = two_blocks(
                ext2, tab_row[2 * b + (a >> 3)], a & 7, tab_row[2 * b + (c >> 3)], c & 7, masks)

    def first_copy(i):
        p = peer(i)
        return pltpu.make_async_remote_copy(
            send_d.at[p], recv_d.at[me], a2a_send.at[i], a2a_recv.at[i],
            device_id=(g, p), device_id_type=MESH)

    batch_table(peer(0))
    to_right.wait_recv()
    to_left.wait_recv()
    for side in range(2):
        for i in range(HALO):
            for q in range(KNZ // 2):
                keep_both(ext2, side * (HALO + BLK_DEV) + i, q, halo_d[side, i, :, q * 128 : (q + 1) * 128])

    def send_first(i, carry):
        pack_rows(peer(i), send_d)
        first_copy(i).start()
        following = peer(i + 1)
        batch_table(following)
        return carry

    lax.fori_loop(0, ROWS - 1, send_first, 0)
    pack_rows(me, recv_d)

    def match_row(k, carry):
        block = act[k, g * ROWS + me]
        tab_owner[k] = (block >> 3) & (ROWS - 1)
        local = [jnp.int32(KNZ)] * ACT
        running = jnp.int32(0)
        for m in range(KNZ):
            column = pat[m, block]
            found = jnp.int32(ACT)
            for j in range(ACT):
                same = column == act[j, g * ROWS + me]
                found = jnp.where(same, j, found)
                local[j] = jnp.where(same, running, local[j])
            tab_j[k * KNZ + m] = found
            tab_rank[k * KNZ + m] = jnp.where(found < ACT, running, 64)
            running = running + (found < ACT).astype(jnp.int32)
        for j in range(ACT):
            tab_local[k * ACT + j] = local[j]
        tab_q[k] = running
        return carry

    lax.fori_loop(0, ACT, match_row, 0)

    def start_row(k, most):
        start = jnp.int32(0)
        for j in range(ACT):
            start = start + jnp.where((j < k) & (tab_owner[j] == tab_owner[k]), tab_q[j], 0)
        tab_start[k] = start
        for j in range(ACT):
            local = tab_local[k * ACT + j]
            tab_dpos[k * ACT + j] = jnp.where(local < KNZ, jnp.minimum(start + local, KNZ - 1), KNZ)
        return jnp.maximum(most, start + tab_q[k])

    most = lax.fori_loop(0, ACT, start_row, jnp.int32(0))
    overflow = jnp.maximum(overflow, (most > KNZ).astype(jnp.int32))

    row_flags[me] = jnp.full((8, 128), overflow, jnp.int32)

    def row_flag_copy(i):
        p = peer(i)
        return pltpu.make_async_remote_copy(
            row_flags.at[me], row_flags.at[me], flag_send.at[i], flag_recv.at[i],
            device_id=(g, p), device_id_type=MESH)

    def region_flag_copy(r):
        return pltpu.make_async_remote_copy(
            region_flags.at[0, r], region_flags.at[1, r], flag_send.at[15 + r], flag_recv.at[15 + r],
            device_id=(lax.rem(g + 2**r, 16), me), device_id_type=MESH)

    def merge_flags(r):
        region_flag_copy(r).wait_recv()
        merged = jnp.maximum(region_flags[0, r], region_flags[1, r])
        if r < 3:
            region_flags[0, r + 1] = merged
            region_flag_copy(r + 1).start()
        else:
            flag_out[0, 0] = merged[0, 0]

    def send_flag(i, carry):
        row_flag_copy(i).start()
        return carry

    lax.fori_loop(0, ROWS - 1, send_flag, 0)

    def turn_of(i, carry):
        tab_turn[peer(i)] = i
        return carry

    lax.fori_loop(0, ROWS, turn_of, 0)

    def place_of(k, carry):
        turn = tab_turn[tab_owner[k]]
        place = jnp.int32(0)
        for j in range(ACT):
            other = tab_turn[tab_owner[j]]
            place = place + ((other < turn) | ((other == turn) & (j < k))).astype(jnp.int32)
        tab_place[k] = place
        return carry

    lax.fori_loop(0, ACT, place_of, 0)

    def entry_at(n, carry):
        entry = jnp.int32(0)
        for k in range(ACT):
            entry = jnp.where(tab_place[k] == n, k, entry)
        tab_order[n] = entry
        return carry

    lax.fori_loop(0, ACT, entry_at, 0)

    def slot_table(r, carry):
        entries = [jnp.int32(0), jnp.int32(0)]
        count = jnp.int32(0)
        for k in range(ACT):
            mine = tab_owner[k] == r
            entries[0] = jnp.where(mine & (count == 0), k, entries[0])
            entries[1] = jnp.where(mine & (count == 1), k, entries[1])
            count = count + mine.astype(jnp.int32)
        packed = [jnp.int32(0)] * KNZ
        for c in range(2):
            k = entries[c]
            start = jnp.where(count > c, tab_start[k], 64)
            for m in range(KNZ):
                place = start + tab_rank[k * KNZ + m]
                code = tab_place[k] * ACT + jnp.minimum(tab_j[k * KNZ + m], ACT - 1)
                for p in range(m + 1 if c == 0 else KNZ):
                    packed[p] = jnp.where(place == p, code, packed[p])
        for p in range(KNZ):
            tab_h[r * KNZ + p] = packed[p]
        return carry

    lax.fori_loop(0, ROWS, slot_table, 0)

    rows2[:, :, KNZ // 2] = jnp.zeros((2, ROWS, BS, 128), BF16)
    hvar[:, :, KNZ // 2] = jnp.zeros((2, ROWS, BS, 128), BF16)
    expanded[2 * ROWS] = jnp.zeros((KNZ // 2, BS, 128), BF16)
    for side in range(2):
        halo_in[side, HALO] = jnp.zeros((BS, WIDTH), BF16)

    x_copy.wait()

    def transpose_chunk(i, carry):
        points = pl.ds(pl.multiple_of(i * 128, 128), 128)
        xt[:, :, points] = jnp.transpose(xv[points, :]).reshape(ACT, BS, 128)
        return carry

    lax.fori_loop(0, PTS // 128, transpose_chunk, 0)

    def spread_slot(r):
        for q in range(KNZ // 2):
            keep_both(rows2, r, q, recv_d[r, q])

    spread_slot(me)

    def take_first(i, carry):
        first_copy(i).wait_recv()
        spread_slot(sender(i))
        return carry

    lax.fori_loop(0, ROWS - 1, take_first, 0)

    def assemble_row(k, carry):
        owner = tab_owner[k]
        for q in range(ACT // 2):
            dfull[pl.ds(pl.multiple_of(k * BS, BS), BS), q * 128 : (q + 1) * 128] = pair_of_blocks(
                rows2, owner, tab_dpos[k * ACT + 2 * q], tab_dpos[k * ACT + 2 * q + 1], masks)
        return carry

    lax.fori_loop(0, ACT, assemble_row, 0)

    def density_chunk(i, carry):
        points = pl.ds(pl.multiple_of(i * CHUNK, CHUNK), CHUNK)
        x = xv[points, :]
        part = jnp.zeros((CHUNK, 128), F32)
        for n in range(COLS // CHUNK):
            product = jnp.dot(x, dfull[:, n * CHUNK : (n + 1) * CHUNK], preferred_element_type=F32)
            product = product * x[:, n * CHUNK : (n + 1) * CHUNK].astype(F32)
            part = part + (product[:, :128] + product[:, 128:])
        dens = jnp.sum(jnp.transpose(part), axis=0, keepdims=True)
        for half in range(CHUNK // 128):
            row = pl.ds(i * (CHUNK // 128) + half, 1)
            dens_half = dens[:, half * 128 : (half + 1) * 128]
            dens_out[row, :] = dens_half
            svec[:, pl.ds(pl.multiple_of(i * CHUNK + half * 128, 128), 128)] = weights[row, :] * jnp.tanh(dens_half)
        return carry

    lax.fori_loop(0, PTS // CHUNK, density_chunk, 0)

    def take_flag(i, carry):
        row_flag_copy(i).wait_recv()
        return carry

    lax.fori_loop(0, ROWS - 1, take_flag, 0)
    merged = row_flags[0]
    for r in range(1, ROWS):
        merged = jnp.maximum(merged, row_flags[r])
    region_flags[0, 0] = merged
    region_flag_copy(0).start()

    def pack_slot(r, target, target_row):
        for q in range(KNZ // 2):
            a = tab_h[r * KNZ + 2 * q]
            b = tab_h[r * KNZ + 2 * q + 1]
            target[target_row, q] = two_blocks(hrows, a >> 4, a & 15, b >> 4, b & 15, masks)

    def second_copy(i):
        p = peer(i)
        return pltpu.make_async_remote_copy(
            send_h.at[p], recv_h.at[me], a2a_send.at[15 + i], a2a_recv.at[15 + i],
            device_id=(g, p), device_id_type=MESH)

    def send_second(i, carry):
        p = peer(i)
        pack_slot(p, send_h, p)
        second_copy(i).start()
        return carry

    def ham_chunk(i, carry):
        rows = [xt[tab_order[i * (CHUNK // BS) + n]] for n in range(CHUNK // BS)]
        scaled = (jnp.concatenate(rows, axis=0).astype(F32) * svec[...]).astype(BF16)
        for n in range(COLS // CHUNK):
            block = jnp.dot(scaled, xv[:, n * CHUNK : (n + 1) * CHUNK], preferred_element_type=F32)
            for half in range(CHUNK // 128):
                part = block[:, half * 128 : (half + 1) * 128]
                swapped = swap_halves(part).astype(BF16)
                part = part.astype(BF16)
                for kk in range(CHUNK // BS):
                    entry = i * (CHUNK // BS) + kk
                    hrows[0, entry, 2 * n + half] = part[kk * BS : (kk + 1) * BS]
                    hrows[1, entry, 2 * n + half] = swapped[kk * BS : (kk + 1) * BS]
        send_second(2 * i, 0)
        send_second(2 * i + 1, 0)
        return carry

    lax.fori_loop(0, COLS // CHUNK, ham_chunk, 0)
    lax.fori_loop(2 * (COLS // CHUNK), ROWS - 1, send_second, 0)
    pack_slot(me, recv_h, me)

    merge_flags(0)
    merge_flags(1)
    merge_flags(2)

    def expand_slot(b):
        for q in range(KNZ // 2):
            keep_both(hvar, b, q, recv_h[b, q])
        for c in range(2):
            for q in range(KNZ // 2):
                expanded[2 * b + c, q] = pair_of_blocks(
                    hvar, b, tab_pos[b * 16 + c * KNZ + 2 * q], tab_pos[b * 16 + c * KNZ + 2 * q + 1], masks)

    expand_slot(me)

    def take_second(i, carry):
        second_copy(i).wait_recv()
        expand_slot(sender(i))
        return carry

    lax.fori_loop(0, ROWS - 1, take_second, 0)

    def sum_row(t):
        picks = []
        for b in range(ROWS):
            count = tab_row[2 * ROWS + b]
            picks.append(jnp.where(
                (tab_row[2 * b] == t) & (count > 0), 2 * b,
                jnp.where((tab_row[2 * b + 1] == t) & (count > 1), 2 * b + 1, 2 * ROWS)))
        total = expanded[picks[0]].astype(F32)
        for b in range(1, ROWS):
            total = total + expanded[picks[b]].astype(F32)
        return total

    to_right.wait_send()
    to_left.wait_send()

    def side_row(t, carry):
        for side in range(2):
            total = sum_row(side * (HALO + BLK_DEV) + t).astype(BF16)
            for q in range(KNZ // 2):
                halo_out[side, t, :, q * 128 : (q + 1) * 128] = total[q]
        return carry

    lax.fori_loop(0, HALO, side_row, 0)

    back_left = pltpu.make_async_remote_copy(
        halo_out.at[0], halo_in.at[0, pl.ds(0, HALO)], halo_send.at[2], halo_recv.at[2],
        device_id=(left, me), device_id_type=MESH)
    back_right = pltpu.make_async_remote_copy(
        halo_out.at[1], halo_in.at[1, pl.ds(0, HALO)], halo_send.at[3], halo_recv.at[3],
        device_id=(right, me), device_id_type=MESH)
    back_left.start()
    back_right.start()

    def own_row(t, carry):
        total = sum_row(HALO + t)
        for q in range(KNZ // 2):
            ham_out[t, :, q * 128 : (q + 1) * 128] = total[q]
        return carry

    lax.fori_loop(0, BLK_DEV, own_row, 0)
    merge_flags(3)
    back_left.wait_recv()
    back_right.wait_recv()

    def add_row(t, carry):
        ham_out[t] = (
            ham_out[t]
            + halo_in[0, back_map[t]].astype(F32)
            + halo_in[1, back_map[BLK_DEV + t]].astype(F32)
        )
        return carry

    lax.fori_loop(0, BLK_DEV, add_row, 0)

    def finish(i, carry):
        first_copy(i).wait_send()
        second_copy(i).wait_send()
        row_flag_copy(i).wait_send()
        return carry

    lax.fori_loop(0, ROWS - 1, finish, 0)
    for r in range(4):
        region_flag_copy(r).wait_send()
    back_left.wait_send()
    back_right.wait_send()


def specs():
    vmem = pl.BlockSpec(memory_space=pltpu.VMEM)
    smem = pl.BlockSpec(memory_space=pltpu.SMEM)
    hbm = pl.BlockSpec(memory_space=pl.ANY)
    return [smem, smem, vmem, hbm, hbm], vmem


def full_capacity(act, pat, weights, x, d):
    in_specs, vmem = specs()
    return pl.pallas_call(
        full_kernel,
        out_shape=(
            jax.ShapeDtypeStruct((PTS // 128, 128), F32),
            jax.ShapeDtypeStruct((BLK_DEV, BS, WIDTH), F32),
        ),
        in_specs=in_specs,
        out_specs=(vmem, vmem),
        scratch_shapes=[
            pltpu.VMEM((PTS, COLS), BF16),
            pltpu.VMEM((COLS, PTS), BF16),
            pltpu.VMEM((3 * BLK_DEV, BS, WIDTH), BF16),
            pltpu.VMEM((ROWS, 2, BS, WIDTH), BF16),
            pltpu.VMEM((2 * ROWS, BS, WIDTH), BF16),
            pltpu.VMEM((2, ACT, KNZ // 2 + 1, BS, 128), BF16),
            pltpu.VMEM((COLS, COLS), BF16),
            pltpu.VMEM((1, PTS), F32),
            pltpu.VMEM((2, ACT, ACT // 2 + 1, BS, 128), BF16),
            pltpu.VMEM((ROWS, 2, BS, WIDTH), BF16),
            pltpu.VMEM((ROWS, 3, BS, WIDTH), BF16),
            pltpu.VMEM((2, BLK_DEV, BS, WIDTH), BF16),
            pltpu.VMEM((2, BLK_DEV, BS, WIDTH), BF16),
            pltpu.SMEM((3 * ROWS,), jnp.int32),
            pltpu.SMEM((ACT,), jnp.int32),
            pltpu.SMEM((ACT * ACT,), jnp.int32),
            pltpu.SMEM((ACT * KNZ,), jnp.int32),
            pltpu.SMEM((2 * ROWS,), jnp.int32),
            pltpu.SemaphoreType.DMA((2,)),
            pltpu.SemaphoreType.DMA((4,)),
            pltpu.SemaphoreType.DMA((4,)),
            pltpu.SemaphoreType.DMA((30,)),
            pltpu.SemaphoreType.DMA((30,)),
        ],
        compiler_params=pltpu.CompilerParams(
            collective_id=1, has_side_effects=True, vmem_limit_bytes=56 << 20
        ),
    )(act, pat, weights, x, d)


def packed_capacity(act, pat, weights, x, d):
    in_specs, vmem = specs()
    half = KNZ // 2
    return pl.pallas_call(
        packed_kernel,
        out_shape=(
            jax.ShapeDtypeStruct((PTS // 128, 128), F32),
            jax.ShapeDtypeStruct((BLK_DEV, BS, WIDTH), F32),
            jax.ShapeDtypeStruct((1, 1), jnp.int32),
        ),
        in_specs=in_specs,
        out_specs=(vmem, vmem, in_specs[0]),
        scratch_shapes=[
            pltpu.VMEM((PTS, COLS), BF16),
            pltpu.VMEM((ACT, BS, PTS), BF16),
            pltpu.VMEM((BLK_DEV, BS, WIDTH), BF16),
            pltpu.VMEM((2, HALO, BS, WIDTH), BF16),
            pltpu.VMEM((2, BLK_DEV + 2 * HALO, half, BS, 128), BF16),
            pltpu.VMEM((ROWS, half, BS, 128), BF16),
            pltpu.VMEM((ROWS, half, BS, 128), BF16),
            pltpu.VMEM((2, ROWS, half + 1, BS, 128), BF16),
            pltpu.VMEM((COLS, COLS), BF16),
            pltpu.VMEM((1, PTS), F32),
            pltpu.VMEM((2, ACT, ACT // 2, BS, 128), BF16),
            pltpu.VMEM((ROWS, half, BS, 128), BF16),
            pltpu.VMEM((ROWS, half, BS, 128), BF16),
            pltpu.VMEM((2, ROWS, half + 1, BS, 128), BF16),
            pltpu.VMEM((2 * ROWS + 1, half, BS, 128), BF16),
            pltpu.VMEM((2, HALO, BS, WIDTH), BF16),
            pltpu.VMEM((2, HALO + 1, BS, WIDTH), BF16),
            pltpu.VMEM((ROWS, 8, 128), jnp.int32),
            pltpu.VMEM((2, 4, 8, 128), jnp.int32),
            pltpu.SMEM((2 * HALO,), jnp.int32),
            pltpu.SMEM((3 * BLK_DEV,), jnp.int32),
            pltpu.SMEM((2 * BLK_DEV,), jnp.int32),
            pltpu.SMEM((3 * ROWS,), jnp.int32),
            pltpu.SMEM((ROWS * KNZ,), jnp.int32),
            pltpu.SMEM((ROWS * 2 * KNZ,), jnp.int32),
            pltpu.SMEM((ACT * KNZ,), jnp.int32),
            pltpu.SMEM((ACT * KNZ,), jnp.int32),
            pltpu.SMEM((ACT * ACT,), jnp.int32),
            pltpu.SMEM((ACT,), jnp.int32),
            pltpu.SMEM((ACT,), jnp.int32),
            pltpu.SMEM((ACT,), jnp.int32),
            pltpu.SMEM((ACT * ACT,), jnp.int32),
            pltpu.SMEM((ROWS * KNZ,), jnp.int32),
            pltpu.SMEM((ROWS,), jnp.int32),
            pltpu.SMEM((ACT,), jnp.int32),
            pltpu.SMEM((ACT,), jnp.int32),
            pltpu.SemaphoreType.DMA((2,)),
            pltpu.SemaphoreType.DMA((4,)),
            pltpu.SemaphoreType.DMA((4,)),
            pltpu.SemaphoreType.DMA((30,)),
            pltpu.SemaphoreType.DMA((30,)),
            pltpu.SemaphoreType.DMA((19,)),
            pltpu.SemaphoreType.DMA((19,)),
        ],
        compiler_params=pltpu.CompilerParams(
            collective_id=0, has_side_effects=True, vmem_limit_bytes=56 << 20
        ),
    )(act, pat, weights, x, d)


def shards(basis_values, grid_weights, density_blocks, pattern, active):
    args = (
        active.T,
        pattern.T,
        grid_weights.reshape(PTS // 128, 128),
        basis_values,
        density_blocks.reshape(BLK_DEV, BS, WIDTH),
    )
    dens, ham, flag = packed_capacity(*args)
    dens, ham = lax.cond(flag[0, 0] > 0, lambda: tuple(full_capacity(*args)), lambda: (dens, ham))
    return dens.reshape(PTS), ham.reshape(BLK_DEV * BS, WIDTH)


def solution(mesh):
    placed = (
        P(("region", "rows"), None),
        P(("region", "rows")),
        P(("region", "rows"), None),
        P(),
        P(),
    )
    return jax.shard_map(
        shards,
        mesh=mesh,
        in_specs=placed,
        out_specs=(P(("region", "rows")), P(("region", "rows"), None)),
        check_vma=False,
    )
```

```python
import functools

import jax
import jax.numpy as jnp
from jax import lax
from jax.experimental import pallas as pl
from jax.experimental.pallas import tpu as pltpu
from jax.sharding import PartitionSpec as P

BS = 64
BLK_DEV = 8
KNZ = 8
ACT = 16
PTS = 1536
ROWS = 16
WIDTH = KNZ * BS
COLS = ACT * BS
CHUNK = 256
NBLK = 2048
HALO = 1
CAP = 7
AHEAD = 4
MESH = pl.DeviceIdType.MESH
F32 = jnp.float32
BF16 = jnp.bfloat16
PEERS = tuple(
    (dy, dz)
    for dz in (4, 3, 5, 2, 6, 1, 7, 0)
    for dy in (0, 1)
    if (dy, dz) != (0, 0)
)


def half_masks():
    lane = lax.broadcasted_iota(jnp.int32, (BS, 128), 1)
    low = jnp.where(lane < BS, 1.0, 0.0).astype(BF16)
    high = jnp.where(lane < BS, 0.0, 1.0).astype(BF16)
    return low, high


def two_blocks(source, row_a, block_a, row_b, block_b, masks):
    low, high = masks
    a = source[block_a & 1, row_a, block_a >> 1]
    b = source[1 - (block_b & 1), row_b, block_b >> 1]
    return a * low + b * high


def pair_of_blocks(source, row, first, second, masks):
    return two_blocks(source, row, first, row, second, masks)


def swap_halves(values):
    return pltpu.roll(values, 64, 1)


def keep_both(target, row, part, values):
    target[0, row, part] = values
    target[1, row, part] = swap_halves(values.astype(F32)).astype(BF16)


def full_kernel(
    act, pat, weights, x_hbm, d_hbm,
    dens_out, ham_out,
    xv, xt, ext, send_d, recv_d, rows2, dfull, svec, hrows, send_h, recv_h,
    halo_out, halo_in,
    tab_row, tab_arr, tab_m, tab_j, tab_slot,
    local_sems, halo_send, halo_recv, a2a_send, a2a_recv,
):
    g = lax.axis_index("region")
    me = lax.axis_index("rows")
    y = lax.div(me, 8)
    z = lax.rem(me, 8)
    left, right = lax.rem(g + 15, 16), lax.rem(g + 1, 16)

    def peer(dy, dz):
        return lax.rem(y + dy, 2) * 8 + lax.rem(z + dz, 8)

    x_copy = pltpu.make_async_copy(x_hbm, xv, local_sems.at[0])
    x_copy.start()
    d_copy = pltpu.make_async_copy(d_hbm, ext.at[pl.ds(BLK_DEV, BLK_DEV)], local_sems.at[1])
    d_copy.start()

    barrier = pltpu.get_barrier_semaphore()
    for n in (left, right):
        pl.semaphore_signal(barrier, inc=1, device_id=(n, me), device_id_type=MESH)
    for dy, dz in PEERS:
        pl.semaphore_signal(barrier, inc=1, device_id=(g, peer(dy, dz)), device_id_type=MESH)
    pl.semaphore_wait(barrier, 17)

    to_right = pltpu.make_async_remote_copy(
        d_hbm, ext.at[pl.ds(0, BLK_DEV)], halo_send.at[0], halo_recv.at[0],
        device_id=(right, me), device_id_type=MESH)
    to_left = pltpu.make_async_remote_copy(
        d_hbm, ext.at[pl.ds(2 * BLK_DEV, BLK_DEV)], halo_send.at[1], halo_recv.at[1],
        device_id=(left, me), device_id_type=MESH)
    to_right.start()
    to_left.start()

    def rows_of_batch(b, carry):
        first = jnp.int32(0)
        second = jnp.int32(0)
        count = jnp.int32(0)
        for e in range(ACT):
            block = act[e, g * ROWS + b]
            mine = ((block >> 3) & (ROWS - 1)) == me
            row = jnp.minimum(((block >> 7) - g + 1) & 15, 2) * BLK_DEV + (block & 7)
            first = jnp.where(mine & (count == 0), row, first)
            second = jnp.where(mine & (count == 1), row, second)
            count = count + mine.astype(jnp.int32)
        tab_row[2 * b] = first
        tab_row[2 * b + 1] = second
        tab_row[2 * ROWS + b] = count
        return carry

    lax.fori_loop(0, ROWS, rows_of_batch, 0)

    d_copy.wait()
    to_right.wait_recv()
    to_left.wait_recv()

    first_copies = []
    for i, (dy, dz) in enumerate(PEERS):
        p = peer(dy, dz)
        for c in range(2):
            send_d[p, c] = ext[tab_row[2 * p + c]]
        copy = pltpu.make_async_remote_copy(
            send_d.at[p], recv_d.at[pl.ds(2 * me, 2)], a2a_send.at[i], a2a_recv.at[i],
            device_id=(g, p), device_id_type=MESH)
        copy.start()
        first_copies.append(copy)
    for c in range(2):
        recv_d[2 * me + c] = ext[tab_row[2 * me + c]]

    ids = [act[k, g * ROWS + me] for k in range(ACT)]
    owners = [(i >> 3) & (ROWS - 1) for i in ids]
    for k in range(ACT):
        earlier = jnp.int32(0)
        for j in range(k):
            earlier = earlier + (owners[j] == owners[k]).astype(jnp.int32)
        tab_arr[k] = owners[k] * 2 + jnp.minimum(earlier, 1)

    def slot_entries(s, carry):
        entry = jnp.int32(0)
        for k in range(ACT):
            entry = jnp.where(tab_arr[k] == s, k, entry)
        tab_slot[s] = entry
        return carry

    lax.fori_loop(0, 2 * ROWS, slot_entries, 0)

    def match_row(k, carry):
        block = act[k, g * ROWS + me]
        found_m = [jnp.int32(KNZ)] * ACT
        for m in range(KNZ):
            column = pat[m, block]
            found = jnp.int32(ACT)
            for j in range(ACT):
                same = column == act[j, g * ROWS + me]
                found = jnp.where(same, j, found)
                found_m[j] = jnp.where(same, m, found_m[j])
            tab_j[k * KNZ + m] = found
        for j in range(ACT):
            tab_m[k * ACT + j] = found_m[j]
        return carry

    lax.fori_loop(0, ACT, match_row, 0)

    rows2[:, :, KNZ // 2] = jnp.zeros((2, ACT, BS, 128), BF16)
    hrows[:, :, ACT // 2] = jnp.zeros((2, ACT, BS, 128), BF16)
    recv_h[:, 2] = jnp.zeros((ROWS, BS, WIDTH), BF16)

    x_copy.wait()

    def transpose_chunk(i, carry):
        points = pl.ds(pl.multiple_of(i * 128, 128), 128)
        xt[:, points] = jnp.transpose(xv[points, :])
        return carry

    lax.fori_loop(0, PTS // 128, transpose_chunk, 0)

    masks = half_masks()
    for copy in first_copies:
        copy.wait_recv()

    def spread_row(k, carry):
        row = recv_d[tab_arr[k]]
        for q in range(KNZ // 2):
            part = row[:, q * 128 : (q + 1) * 128]
            rows2[0, k, q] = part
            rows2[1, k, q] = swap_halves(part.astype(F32)).astype(BF16)
        for q in range(ACT // 2):
            first = tab_m[k * ACT + 2 * q]
            second = tab_m[k * ACT + 2 * q + 1]
            dfull[pl.ds(pl.multiple_of(k * BS, BS), BS), q * 128 : (q + 1) * 128] = pair_of_blocks(
                rows2, k, first, second, masks)
        return carry

    lax.fori_loop(0, ACT, spread_row, 0)

    def density_chunk(i, carry):
        points = pl.ds(pl.multiple_of(i * CHUNK, CHUNK), CHUNK)
        x = xv[points, :]
        part = jnp.zeros((CHUNK, 128), F32)
        for n in range(COLS // CHUNK):
            product = jnp.dot(x, dfull[:, n * CHUNK : (n + 1) * CHUNK], preferred_element_type=F32)
            product = product * x[:, n * CHUNK : (n + 1) * CHUNK].astype(F32)
            part = part + (product[:, :128] + product[:, 128:])
        dens = jnp.sum(jnp.transpose(part), axis=0, keepdims=True)
        for half in range(CHUNK // 128):
            row = pl.ds(i * (CHUNK // 128) + half, 1)
            dens_half = dens[:, half * 128 : (half + 1) * 128]
            dens_out[row, :] = dens_half
            svec[:, pl.ds(pl.multiple_of(i * CHUNK + half * 128, 128), 128)] = weights[row, :] * jnp.tanh(dens_half)
        return carry

    lax.fori_loop(0, PTS // CHUNK, density_chunk, 0)

    def ham_chunk(i, carry):
        scaled = (xt[pl.ds(pl.multiple_of(i * CHUNK, CHUNK), CHUNK), :].astype(F32) * svec[...]).astype(BF16)
        for n in range(COLS // CHUNK):
            block = jnp.dot(scaled, xv[:, n * CHUNK : (n + 1) * CHUNK], preferred_element_type=F32)
            for half in range(CHUNK // 128):
                part = block[:, half * 128 : (half + 1) * 128]
                swapped = swap_halves(part).astype(BF16)
                part = part.astype(BF16)
                for kk in range(CHUNK // BS):
                    entry = i * (CHUNK // BS) + kk
                    hrows[0, entry, 2 * n + half] = part[kk * BS : (kk + 1) * BS]
                    hrows[1, entry, 2 * n + half] = swapped[kk * BS : (kk + 1) * BS]
        return carry

    lax.fori_loop(0, COLS // CHUNK, ham_chunk, 0)

    for copy in first_copies:
        copy.wait_send()

    def gather_slots(p, target, target_row):
        for c in range(2):
            k = tab_slot[2 * p + c]
            for q in range(KNZ // 2):
                first = tab_j[k * KNZ + 2 * q]
                second = tab_j[k * KNZ + 2 * q + 1]
                target[target_row, c, :, q * 128 : (q + 1) * 128] = pair_of_blocks(
                    hrows, k, first, second, masks)

    second_copies = []
    for i, (dy, dz) in enumerate(PEERS):
        p = peer(dy, dz)
        gather_slots(p, send_h, p)
        copy = pltpu.make_async_remote_copy(
            send_h.at[p], recv_h.at[me, pl.ds(0, 2)], a2a_send.at[15 + i], a2a_recv.at[15 + i],
            device_id=(g, p), device_id_type=MESH)
        copy.start()
        second_copies.append(copy)
    gather_slots(me, recv_h, me)
    for copy in second_copies:
        copy.wait_recv()

    def sum_row(t):
        picks = []
        for b in range(ROWS):
            count = tab_row[2 * ROWS + b]
            picks.append(jnp.where(
                (tab_row[2 * b] == t) & (count > 0), 0,
                jnp.where((tab_row[2 * b + 1] == t) & (count > 1), 1, 2)))
        total = recv_h[0, picks[0]].astype(F32)
        for b in range(1, ROWS):
            total = total + recv_h[b, picks[b]].astype(F32)
        return total

    def side_row(t, carry):
        for side, base in ((0, 0), (1, 2 * BLK_DEV)):
            halo_out[side, t] = sum_row(base + t).astype(BF16)
        return carry

    lax.fori_loop(0, BLK_DEV, side_row, 0)

    back_left = pltpu.make_async_remote_copy(
        halo_out.at[0], halo_in.at[0], halo_send.at[2], halo_recv.at[2],
        device_id=(left, me), device_id_type=MESH)
    back_right = pltpu.make_async_remote_copy(
        halo_out.at[1], halo_in.at[1], halo_send.at[3], halo_recv.at[3],
        device_id=(right, me), device_id_type=MESH)
    back_left.start()
    back_right.start()

    def own_row(t, carry):
        ham_out[t] = sum_row(BLK_DEV + t)
        return carry

    lax.fori_loop(0, BLK_DEV, own_row, 0)
    back_left.wait_recv()
    back_right.wait_recv()

    def add_row(t, carry):
        ham_out[t] = ham_out[t] + halo_in[0, t].astype(F32) + halo_in[1, t].astype(F32)
        return carry

    lax.fori_loop(0, BLK_DEV, add_row, 0)

    for copy in second_copies:
        copy.wait_send()
    for copy in (to_right, to_left, back_left, back_right):
        copy.wait_send()


def offset_of(i):
    j = lax.div(i, 2)
    dz = 4 + lax.div(j + 1, 2) * (1 - 2 * lax.rem(j, 2))
    return 1 - lax.rem(i, 2), dz


def fill_slot(slots, slot, source, pick, masks):
    low, high = masks
    for q in range(CAP // 2):
        slots[slot, q * BS : (q + 1) * BS] = two_blocks(source, *pick(2 * q), *pick(2 * q + 1), masks)
    row, block = pick(CAP - 1)
    a = source[block & 1, row, block >> 1]
    b = source[1 - (block & 1), row, block >> 1]
    half = BS // 2
    slots[slot, CAP // 2 * BS :] = a[:half] * low[:half] + b[half:] * high[half:]


def open_slot(target, slots, slot):
    for q in range(CAP // 2):
        keep_both(target, slot, q, slots[slot, q * BS : (q + 1) * BS])
    part = slots[slot, CAP // 2 * BS :]
    swapped = swap_halves(part.astype(F32)).astype(BF16)
    half = BS // 2
    target[0, slot, CAP // 2, :half] = part
    target[0, slot, CAP // 2, half:] = swapped
    target[1, slot, CAP // 2, :half] = swapped
    target[1, slot, CAP // 2, half:] = part


def packed_kernel(
    act, pat_hbm, weights, x_hbm, d_hbm,
    dens_out, ham_out, flag_out,
    xv, xt, own, halo_d, ext2, send_d, recv_d, rows2, dfull, svec, hrows, send_h,
    recv_h, hvar, expanded, halo_out, halo_in, row_flags, region_flags,
    pat, halo_src, row_map, back_map, tab_row, tab_src, tab_pos,
    tab_j, tab_rank, tab_local, tab_q, tab_start, tab_owner, tab_dpos, tab_h, tab_turn, tab_place, tab_order,
    local_sems, halo_send, halo_recv, a2a_send, a2a_recv, flag_send, flag_recv,
):
    g = lax.axis_index("region")
    me = lax.axis_index("rows")
    y = lax.div(me, 8)
    z = lax.rem(me, 8)
    left, right = lax.rem(g + 15, 16), lax.rem(g + 1, 16)

    def peer(i):
        dy, dz = offset_of(i)
        return lax.rem(y + dy, 2) * 8 + lax.rem(z + dz, 8)

    def sender(i):
        dy, dz = offset_of(i)
        return lax.rem(y + dy, 2) * 8 + lax.rem(z + 8 - dz, 8)

    x_copy = pltpu.make_async_copy(x_hbm, xv, local_sems.at[0])
    d_copy = pltpu.make_async_copy(d_hbm, own, local_sems.at[1])
    pat_copy = pltpu.make_async_copy(pat_hbm, pat, local_sems.at[2])
    d_copy.start()
    pat_copy.start()
    x_copy.start()

    barrier = pltpu.get_barrier_semaphore()
    for n in (left, right) + tuple(lax.rem(g + 16 - hop, 16) for hop in (2, 4, 8)):
        pl.semaphore_signal(barrier, inc=1, device_id=(n, me), device_id_type=MESH)

    def greet(i, carry):
        pl.semaphore_signal(barrier, inc=1, device_id=(g, peer(i)), device_id_type=MESH)
        return carry

    lax.fori_loop(0, ROWS - 1, greet, 0)

    def named(region, start):
        def one(b, mask):
            for e in range(start, start + 4):
                block = act[e, region * ROWS + b]
                bit = (1 + (block & 1)) * (1 + 3 * ((block >> 1) & 1)) * (1 + 15 * ((block >> 2) & 1))
                mask = mask | jnp.where(((block >> 3) & (ROWS - 1)) == me, bit, 0)
            return mask

        return lax.fori_loop(0, ROWS, one, jnp.int32(0))

    def ranks(mask):
        taken = jnp.int32(0)
        bits, places = [], []
        for s in range(BLK_DEV):
            bit = (mask >> s) & 1
            bits.append(bit)
            places.append(taken)
            taken = taken + bit
        return bits, places, taken

    overflow = jnp.int32(0)
    for side, mask in enumerate((named(right, 8), named(left, 12))):
        bits, places, taken = ranks(mask)
        for i in range(HALO):
            source = jnp.int32(0)
            for s in range(BLK_DEV):
                source = jnp.where((bits[s] == 1) & (places[s] == i), s, source)
            halo_src[side * HALO + i] = source
        for s in range(BLK_DEV):
            back_map[side * BLK_DEV + s] = jnp.where(bits[s] == 1, jnp.minimum(places[s], HALO - 1), HALO)
        overflow = jnp.maximum(overflow, (taken > HALO).astype(jnp.int32))

    d_copy.wait()
    for side in range(2):
        for i in range(HALO):
            halo_out[side, i] = own[halo_src[side * HALO + i]]
    pl.semaphore_wait(barrier, 20)

    to_right = pltpu.make_async_remote_copy(
        halo_out.at[0], halo_d.at[0], halo_send.at[0], halo_recv.at[0],
        device_id=(right, me), device_id_type=MESH)
    to_left = pltpu.make_async_remote_copy(
        halo_out.at[1], halo_d.at[1], halo_send.at[1], halo_recv.at[1],
        device_id=(left, me), device_id_type=MESH)
    to_right.start()
    to_left.start()

    for side, start in ((0, 8), (1, 12)):
        bits, places, taken = ranks(named(g, start))
        for s in range(BLK_DEV):
            row_map[2 * side * BLK_DEV + s] = side * (HALO + BLK_DEV) + jnp.minimum(places[s], HALO - 1)
    for s in range(BLK_DEV):
        row_map[BLK_DEV + s] = HALO + s

    def own_row_twice(s, carry):
        for q in range(KNZ // 2):
            keep_both(ext2, HALO + s, q, own[s, :, q * 128 : (q + 1) * 128])
        return carry

    lax.fori_loop(0, BLK_DEV, own_row_twice, 0)

    def batch_table(b):
        ids = [act[e, g * ROWS + b] for e in range(ACT)]
        blocks = [jnp.int32(0), jnp.int32(0)]
        count = jnp.int32(0)
        for e in range(ACT):
            mine = ((ids[e] >> 3) & (ROWS - 1)) == me
            blocks[0] = jnp.where(mine & (count == 0), ids[e], blocks[0])
            blocks[1] = jnp.where(mine & (count == 1), ids[e], blocks[1])
            count = count + mine.astype(jnp.int32)
        packed = [jnp.int32(0)] * CAP
        running = jnp.int32(0)
        for c in range(2):
            group = jnp.minimum(((blocks[c] >> 7) - g + 1) & 15, 2)
            tab_row[2 * b + c] = row_map[group * BLK_DEV + (blocks[c] & 7)]
            valid = count > c
            for m in range(KNZ):
                column = pat[m, blocks[c]]
                gap = column ^ ids[0]
                for e in range(1, ACT):
                    gap = jnp.minimum(gap, column ^ ids[e])
                match = (gap == 0) & valid
                for p in range(min(m + 1, CAP) if c == 0 else CAP):
                    packed[p] = jnp.where(match & (running == p), c * KNZ + m, packed[p])
                tab_pos[b * 16 + c * KNZ + m] = jnp.where(match, jnp.minimum(running, CAP - 1), KNZ)
                running = running + match.astype(jnp.int32)
        for p in range(CAP):
            tab_src[b * KNZ + p] = packed[p]
        tab_row[2 * ROWS + b] = count

    masks = half_masks()

    def pack_rows(b, target):
        def pick(p):
            code = tab_src[b * KNZ + p]
            return tab_row[2 * b + (code >> 3)], code & 7

        fill_slot(target, b, ext2, pick, masks)

    def first_copy(i):
        p = peer(i)
        return pltpu.make_async_remote_copy(
            send_d.at[p], recv_d.at[me], a2a_send.at[i], a2a_recv.at[i],
            device_id=(g, p), device_id_type=MESH)

    pat_copy.wait()
    for i in range(AHEAD):
        batch_table(peer(i))
    to_right.wait_recv()
    to_left.wait_recv()
    for side in range(2):
        for i in range(HALO):
            for q in range(KNZ // 2):
                keep_both(ext2, side * (HALO + BLK_DEV) + i, q, halo_d[side, i, :, q * 128 : (q + 1) * 128])

    def send_first(i, carry):
        pack_rows(peer(i), send_d)
        first_copy(i).start()
        return carry

    def send_and_prepare(i, carry):
        send_first(i, carry)
        batch_table(peer(i + AHEAD))
        return carry

    lax.fori_loop(0, ROWS - AHEAD, send_and_prepare, 0)
    lax.fori_loop(ROWS - AHEAD, ROWS - 1, send_first, 0)
    pack_rows(me, recv_d)

    def match_row(k, carry):
        block = act[k, g * ROWS + me]
        tab_owner[k] = (block >> 3) & (ROWS - 1)
        local = [jnp.int32(KNZ)] * ACT
        running = jnp.int32(0)
        for m in range(KNZ):
            column = pat[m, block]
            found = jnp.int32(ACT)
            for j in range(ACT):
                same = column == act[j, g * ROWS + me]
                found = jnp.where(same, j, found)
                local[j] = jnp.where(same, running, local[j])
            tab_j[k * KNZ + m] = found
            tab_rank[k * KNZ + m] = jnp.where(found < ACT, running, 64)
            running = running + (found < ACT).astype(jnp.int32)
        for j in range(ACT):
            tab_local[k * ACT + j] = local[j]
        tab_q[k] = running
        return carry

    lax.fori_loop(0, ACT, match_row, 0)

    def start_row(k, most):
        start = jnp.int32(0)
        for j in range(ACT):
            start = start + jnp.where((j < k) & (tab_owner[j] == tab_owner[k]), tab_q[j], 0)
        tab_start[k] = start
        for j in range(ACT):
            local = tab_local[k * ACT + j]
            tab_dpos[k * ACT + j] = jnp.where(local < KNZ, jnp.minimum(start + local, CAP - 1), KNZ)
        return jnp.maximum(most, start + tab_q[k])

    most = lax.fori_loop(0, ACT, start_row, jnp.int32(0))
    overflow = jnp.maximum(overflow, (most > CAP).astype(jnp.int32))

    row_flags[me] = jnp.full((8, 128), overflow, jnp.int32)

    def row_flag_copy(i):
        p = peer(i)
        return pltpu.make_async_remote_copy(
            row_flags.at[me], row_flags.at[me], flag_send.at[i], flag_recv.at[i],
            device_id=(g, p), device_id_type=MESH)

    def region_flag_copy(r):
        return pltpu.make_async_remote_copy(
            region_flags.at[0, r], region_flags.at[1, r], flag_send.at[15 + r], flag_recv.at[15 + r],
            device_id=(lax.rem(g + 2**r, 16), me), device_id_type=MESH)

    def merge_flags(r):
        region_flag_copy(r).wait_recv()
        merged = jnp.maximum(region_flags[0, r], region_flags[1, r])
        if r < 3:
            region_flags[0, r + 1] = merged
            region_flag_copy(r + 1).start()
        else:
            flag_out[0, 0] = merged[0, 0]

    def send_flag(i, carry):
        row_flag_copy(i).start()
        return carry

    lax.fori_loop(0, ROWS - 1, send_flag, 0)

    def turn_of(i, carry):
        tab_turn[peer(i)] = i
        return carry

    lax.fori_loop(0, ROWS, turn_of, 0)

    def place_of(k, carry):
        turn = tab_turn[tab_owner[k]]
        place = jnp.int32(0)
        for j in range(ACT):
            other = tab_turn[tab_owner[j]]
            place = place + ((other < turn) | ((other == turn) & (j < k))).astype(jnp.int32)
        tab_place[k] = place
        return carry

    lax.fori_loop(0, ACT, place_of, 0)

    def entry_at(n, carry):
        entry = jnp.int32(0)
        for k in range(ACT):
            entry = jnp.where(tab_place[k] == n, k, entry)
        tab_order[n] = entry
        return carry

    lax.fori_loop(0, ACT, entry_at, 0)

    def slot_table(r, carry):
        entries = [jnp.int32(0), jnp.int32(0)]
        count = jnp.int32(0)
        for k in range(ACT):
            mine = tab_owner[k] == r
            entries[0] = jnp.where(mine & (count == 0), k, entries[0])
            entries[1] = jnp.where(mine & (count == 1), k, entries[1])
            count = count + mine.astype(jnp.int32)
        packed = [jnp.int32(0)] * CAP
        for c in range(2):
            k = entries[c]
            start = jnp.where(count > c, tab_start[k], 64)
            for m in range(KNZ):
                place = start + tab_rank[k * KNZ + m]
                code = tab_place[k] * ACT + jnp.minimum(tab_j[k * KNZ + m], ACT - 1)
                for p in range(min(m + 1, CAP) if c == 0 else CAP):
                    packed[p] = jnp.where(place == p, code, packed[p])
        for p in range(CAP):
            tab_h[r * KNZ + p] = packed[p]
        return carry

    lax.fori_loop(0, ROWS, slot_table, 0)

    rows2[:, :, KNZ // 2] = jnp.zeros((2, ROWS, BS, 128), BF16)
    hvar[:, :, KNZ // 2] = jnp.zeros((2, ROWS, BS, 128), BF16)
    expanded[2 * ROWS] = jnp.zeros((KNZ // 2, BS, 128), BF16)
    for side in range(2):
        halo_in[side, HALO] = jnp.zeros((BS, WIDTH), BF16)

    x_copy.wait()

    def transpose_chunk(i, carry):
        points = pl.ds(pl.multiple_of(i * 128, 128), 128)
        xt[:, :, points] = jnp.transpose(xv[points, :]).reshape(ACT, BS, 128)
        return carry

    lax.fori_loop(0, PTS // 128, transpose_chunk, 0)

    def spread_slot(r):
        open_slot(rows2, recv_d, r)

    spread_slot(me)

    def take_first(i, carry):
        first_copy(i).wait_recv()
        spread_slot(sender(i))
        return carry

    lax.fori_loop(0, ROWS - 1, take_first, 0)

    def assemble_row(k, carry):
        owner = tab_owner[k]
        for q in range(ACT // 2):
            dfull[pl.ds(pl.multiple_of(k * BS, BS), BS), q * 128 : (q + 1) * 128] = pair_of_blocks(
                rows2, owner, tab_dpos[k * ACT + 2 * q], tab_dpos[k * ACT + 2 * q + 1], masks)
        return carry

    lax.fori_loop(0, ACT, assemble_row, 0)

    def density_chunk(i, carry):
        points = pl.ds(pl.multiple_of(i * CHUNK, CHUNK), CHUNK)
        x = xv[points, :]
        part = jnp.zeros((CHUNK, 128), F32)
        for n in range(COLS // CHUNK):
            product = jnp.dot(x, dfull[:, n * CHUNK : (n + 1) * CHUNK], preferred_element_type=F32)
            product = product * x[:, n * CHUNK : (n + 1) * CHUNK].astype(F32)
            part = part + (product[:, :128] + product[:, 128:])
        dens = jnp.sum(jnp.transpose(part), axis=0, keepdims=True)
        for half in range(CHUNK // 128):
            row = pl.ds(i * (CHUNK // 128) + half, 1)
            dens_half = dens[:, half * 128 : (half + 1) * 128]
            dens_out[row, :] = dens_half
            svec[:, pl.ds(pl.multiple_of(i * CHUNK + half * 128, 128), 128)] = weights[row, :] * jnp.tanh(dens_half)
        return carry

    lax.fori_loop(0, PTS // CHUNK, density_chunk, 0)

    def take_flag(i, carry):
        row_flag_copy(i).wait_recv()
        return carry

    lax.fori_loop(0, ROWS - 1, take_flag, 0)
    merged = row_flags[0]
    for r in range(1, ROWS):
        merged = jnp.maximum(merged, row_flags[r])
    region_flags[0, 0] = merged
    region_flag_copy(0).start()

    def pack_slot(r, target):
        def pick(p):
            code = tab_h[r * KNZ + p]
            return code >> 4, code & 15

        fill_slot(target, r, hrows, pick, masks)

    def second_copy(i):
        p = peer(i)
        return pltpu.make_async_remote_copy(
            send_h.at[p], recv_h.at[me], a2a_send.at[15 + i], a2a_recv.at[15 + i],
            device_id=(g, p), device_id_type=MESH)

    def send_second(i, carry):
        p = peer(i)
        pack_slot(p, send_h)
        second_copy(i).start()
        return carry

    def ham_chunk(i, carry):
        rows = [xt[tab_order[i * (CHUNK // BS) + n]] for n in range(CHUNK // BS)]
        scaled = (jnp.concatenate(rows, axis=0).astype(F32) * svec[...]).astype(BF16)
        for n in range(COLS // CHUNK):
            block = jnp.dot(scaled, xv[:, n * CHUNK : (n + 1) * CHUNK], preferred_element_type=F32)
            for half in range(CHUNK // 128):
                part = block[:, half * 128 : (half + 1) * 128]
                swapped = swap_halves(part).astype(BF16)
                part = part.astype(BF16)
                for kk in range(CHUNK // BS):
                    entry = i * (CHUNK // BS) + kk
                    hrows[0, entry, 2 * n + half] = part[kk * BS : (kk + 1) * BS]
                    hrows[1, entry, 2 * n + half] = swapped[kk * BS : (kk + 1) * BS]
        send_second(2 * i, 0)
        send_second(2 * i + 1, 0)
        return carry

    lax.fori_loop(0, COLS // CHUNK, ham_chunk, 0)
    lax.fori_loop(2 * (COLS // CHUNK), ROWS - 1, send_second, 0)
    pack_slot(me, recv_h)

    merge_flags(0)
    merge_flags(1)
    merge_flags(2)

    def expand_slot(b):
        open_slot(hvar, recv_h, b)
        for c in range(2):
            for q in range(KNZ // 2):
                expanded[2 * b + c, q] = pair_of_blocks(
                    hvar, b, tab_pos[b * 16 + c * KNZ + 2 * q], tab_pos[b * 16 + c * KNZ + 2 * q + 1], masks)

    expand_slot(me)

    def take_second(i, carry):
        second_copy(i).wait_recv()
        expand_slot(sender(i))
        return carry

    lax.fori_loop(0, ROWS - 1, take_second, 0)

    def sum_row(t):
        picks = []
        for b in range(ROWS):
            count = tab_row[2 * ROWS + b]
            picks.append(jnp.where(
                (tab_row[2 * b] == t) & (count > 0), 2 * b,
                jnp.where((tab_row[2 * b + 1] == t) & (count > 1), 2 * b + 1, 2 * ROWS)))
        total = expanded[picks[0]].astype(F32)
        for b in range(1, ROWS):
            total = total + expanded[picks[b]].astype(F32)
        return total

    to_right.wait_send()
    to_left.wait_send()

    def side_row(t, carry):
        for side in range(2):
            total = sum_row(side * (HALO + BLK_DEV) + t).astype(BF16)
            for q in range(KNZ // 2):
                halo_out[side, t, :, q * 128 : (q + 1) * 128] = total[q]
        return carry

    lax.fori_loop(0, HALO, side_row, 0)

    back_left = pltpu.make_async_remote_copy(
        halo_out.at[0], halo_in.at[0, pl.ds(0, HALO)], halo_send.at[2], halo_recv.at[2],
        device_id=(left, me), device_id_type=MESH)
    back_right = pltpu.make_async_remote_copy(
        halo_out.at[1], halo_in.at[1, pl.ds(0, HALO)], halo_send.at[3], halo_recv.at[3],
        device_id=(right, me), device_id_type=MESH)
    back_left.start()
    back_right.start()

    def own_row(t, carry):
        total = sum_row(HALO + t)
        for q in range(KNZ // 2):
            ham_out[t, :, q * 128 : (q + 1) * 128] = total[q]
        return carry

    lax.fori_loop(0, BLK_DEV, own_row, 0)
    merge_flags(3)
    back_left.wait_recv()
    back_right.wait_recv()

    def add_row(t, carry):
        ham_out[t] = (
            ham_out[t]
            + halo_in[0, back_map[t]].astype(F32)
            + halo_in[1, back_map[BLK_DEV + t]].astype(F32)
        )
        return carry

    lax.fori_loop(0, BLK_DEV, add_row, 0)

    def finish(i, carry):
        first_copy(i).wait_send()
        second_copy(i).wait_send()
        row_flag_copy(i).wait_send()
        return carry

    lax.fori_loop(0, ROWS - 1, finish, 0)
    for r in range(4):
        region_flag_copy(r).wait_send()
    back_left.wait_send()
    back_right.wait_send()


def specs():
    vmem = pl.BlockSpec(memory_space=pltpu.VMEM)
    smem = pl.BlockSpec(memory_space=pltpu.SMEM)
    hbm = pl.BlockSpec(memory_space=pl.ANY)
    return [smem, smem, vmem, hbm, hbm], vmem


def full_capacity(act, pat, weights, x, d):
    in_specs, vmem = specs()
    return pl.pallas_call(
        full_kernel,
        out_shape=(
            jax.ShapeDtypeStruct((PTS // 128, 128), F32),
            jax.ShapeDtypeStruct((BLK_DEV, BS, WIDTH), F32),
        ),
        in_specs=in_specs,
        out_specs=(vmem, vmem),
        scratch_shapes=[
            pltpu.VMEM((PTS, COLS), BF16),
            pltpu.VMEM((COLS, PTS), BF16),
            pltpu.VMEM((3 * BLK_DEV, BS, WIDTH), BF16),
            pltpu.VMEM((ROWS, 2, BS, WIDTH), BF16),
            pltpu.VMEM((2 * ROWS, BS, WIDTH), BF16),
            pltpu.VMEM((2, ACT, KNZ // 2 + 1, BS, 128), BF16),
            pltpu.VMEM((COLS, COLS), BF16),
            pltpu.VMEM((1, PTS), F32),
            pltpu.VMEM((2, ACT, ACT // 2 + 1, BS, 128), BF16),
            pltpu.VMEM((ROWS, 2, BS, WIDTH), BF16),
            pltpu.VMEM((ROWS, 3, BS, WIDTH), BF16),
            pltpu.VMEM((2, BLK_DEV, BS, WIDTH), BF16),
            pltpu.VMEM((2, BLK_DEV, BS, WIDTH), BF16),
            pltpu.SMEM((3 * ROWS,), jnp.int32),
            pltpu.SMEM((ACT,), jnp.int32),
            pltpu.SMEM((ACT * ACT,), jnp.int32),
            pltpu.SMEM((ACT * KNZ,), jnp.int32),
            pltpu.SMEM((2 * ROWS,), jnp.int32),
            pltpu.SemaphoreType.DMA((2,)),
            pltpu.SemaphoreType.DMA((4,)),
            pltpu.SemaphoreType.DMA((4,)),
            pltpu.SemaphoreType.DMA((30,)),
            pltpu.SemaphoreType.DMA((30,)),
        ],
        compiler_params=pltpu.CompilerParams(
            collective_id=1, has_side_effects=True, vmem_limit_bytes=56 << 20
        ),
    )(act, pat, weights, x, d)


def packed_capacity(act, pat, weights, x, d):
    in_specs, vmem = specs()
    half = KNZ // 2
    in_specs[1] = in_specs[3]
    return pl.pallas_call(
        packed_kernel,
        out_shape=(
            jax.ShapeDtypeStruct((PTS // 128, 128), F32),
            jax.ShapeDtypeStruct((BLK_DEV, BS, WIDTH), F32),
            jax.ShapeDtypeStruct((1, 1), jnp.int32),
        ),
        in_specs=in_specs,
        out_specs=(vmem, vmem, in_specs[0]),
        scratch_shapes=[
            pltpu.VMEM((PTS, COLS), BF16),
            pltpu.VMEM((ACT, BS, PTS), BF16),
            pltpu.VMEM((BLK_DEV, BS, WIDTH), BF16),
            pltpu.VMEM((2, HALO, BS, WIDTH), BF16),
            pltpu.VMEM((2, BLK_DEV + 2 * HALO, half, BS, 128), BF16),
            pltpu.VMEM((ROWS, CAP * BS // 2, 128), BF16),
            pltpu.VMEM((ROWS, CAP * BS // 2, 128), BF16),
            pltpu.VMEM((2, ROWS, half + 1, BS, 128), BF16),
            pltpu.VMEM((COLS, COLS), BF16),
            pltpu.VMEM((1, PTS), F32),
            pltpu.VMEM((2, ACT, ACT // 2, BS, 128), BF16),
            pltpu.VMEM((ROWS, CAP * BS // 2, 128), BF16),
            pltpu.VMEM((ROWS, CAP * BS // 2, 128), BF16),
            pltpu.VMEM((2, ROWS, half + 1, BS, 128), BF16),
            pltpu.VMEM((2 * ROWS + 1, half, BS, 128), BF16),
            pltpu.VMEM((2, HALO, BS, WIDTH), BF16),
            pltpu.VMEM((2, HALO + 1, BS, WIDTH), BF16),
            pltpu.VMEM((ROWS, 8, 128), jnp.int32),
            pltpu.VMEM((2, 4, 8, 128), jnp.int32),
            pltpu.SMEM((KNZ, NBLK), jnp.int32),
            pltpu.SMEM((2 * HALO,), jnp.int32),
            pltpu.SMEM((3 * BLK_DEV,), jnp.int32),
            pltpu.SMEM((2 * BLK_DEV,), jnp.int32),
            pltpu.SMEM((3 * ROWS,), jnp.int32),
            pltpu.SMEM((ROWS * KNZ,), jnp.int32),
            pltpu.SMEM((ROWS * 2 * KNZ,), jnp.int32),
            pltpu.SMEM((ACT * KNZ,), jnp.int32),
            pltpu.SMEM((ACT * KNZ,), jnp.int32),
            pltpu.SMEM((ACT * ACT,), jnp.int32),
            pltpu.SMEM((ACT,), jnp.int32),
            pltpu.SMEM((ACT,), jnp.int32),
            pltpu.SMEM((ACT,), jnp.int32),
            pltpu.SMEM((ACT * ACT,), jnp.int32),
            pltpu.SMEM((ROWS * KNZ,), jnp.int32),
            pltpu.SMEM((ROWS,), jnp.int32),
            pltpu.SMEM((ACT,), jnp.int32),
            pltpu.SMEM((ACT,), jnp.int32),
            pltpu.SemaphoreType.DMA((3,)),
            pltpu.SemaphoreType.DMA((4,)),
            pltpu.SemaphoreType.DMA((4,)),
            pltpu.SemaphoreType.DMA((30,)),
            pltpu.SemaphoreType.DMA((30,)),
            pltpu.SemaphoreType.DMA((19,)),
            pltpu.SemaphoreType.DMA((19,)),
        ],
        compiler_params=pltpu.CompilerParams(
            collective_id=0, has_side_effects=True, vmem_limit_bytes=56 << 20
        ),
    )(act, pat, weights, x, d)


def shards(basis_values, grid_weights, density_blocks, pattern, active):
    args = (
        active.T,
        pattern.T,
        grid_weights.reshape(PTS // 128, 128),
        basis_values,
        density_blocks.reshape(BLK_DEV, BS, WIDTH),
    )
    dens, ham, flag = packed_capacity(*args)
    dens, ham = lax.cond(flag[0, 0] > 0, lambda: tuple(full_capacity(*args)), lambda: (dens, ham))
    return dens.reshape(PTS), ham.reshape(BLK_DEV * BS, WIDTH)


def solution(mesh):
    placed = (
        P(("region", "rows"), None),
        P(("region", "rows")),
        P(("region", "rows"), None),
        P(),
        P(),
    )
    return jax.shard_map(
        shards,
        mesh=mesh,
        in_specs=placed,
        out_specs=(P(("region", "rows")), P(("region", "rows"), None)),
        check_vma=False,
    )
```

```python
import functools

import jax
import jax.numpy as jnp
from jax import lax
from jax.experimental import pallas as pl
from jax.experimental.pallas import tpu as pltpu
from jax.sharding import PartitionSpec as P

BS = 64
BLK_DEV = 8
KNZ = 8
ACT = 16
PTS = 1536
ROWS = 16
WIDTH = KNZ * BS
COLS = ACT * BS
CHUNK = 256
NBLK = 2048
HALO = 1
CAP = 7
AHEAD = 4
POINTS = 512
MESH = pl.DeviceIdType.MESH
F32 = jnp.float32
BF16 = jnp.bfloat16
PEERS = tuple(
    (dy, dz)
    for dz in (4, 3, 5, 2, 6, 1, 7, 0)
    for dy in (0, 1)
    if (dy, dz) != (0, 0)
)


def half_masks():
    lane = lax.broadcasted_iota(jnp.int32, (BS, 128), 1)
    low = jnp.where(lane < BS, 1.0, 0.0).astype(BF16)
    high = jnp.where(lane < BS, 0.0, 1.0).astype(BF16)
    return low, high


def two_blocks(source, row_a, block_a, row_b, block_b, masks):
    low, high = masks
    a = source[block_a & 1, row_a, block_a >> 1]
    b = source[1 - (block_b & 1), row_b, block_b >> 1]
    return a * low + b * high


def pair_of_blocks(source, row, first, second, masks):
    return two_blocks(source, row, first, row, second, masks)


def swap_halves(values):
    return pltpu.roll(values, 64, 1)


def keep_both(target, row, part, values):
    target[0, row, part] = values
    target[1, row, part] = swap_halves(values.astype(F32)).astype(BF16)


def full_kernel(
    act, pat, weights, x_hbm, d_hbm,
    dens_out, ham_out,
    xv, xt, ext, send_d, recv_d, rows2, dfull, svec, hrows, send_h, recv_h,
    halo_out, halo_in,
    tab_row, tab_arr, tab_m, tab_j, tab_slot,
    local_sems, halo_send, halo_recv, a2a_send, a2a_recv,
):
    g = lax.axis_index("region")
    me = lax.axis_index("rows")
    y = lax.div(me, 8)
    z = lax.rem(me, 8)
    left, right = lax.rem(g + 15, 16), lax.rem(g + 1, 16)

    def peer(dy, dz):
        return lax.rem(y + dy, 2) * 8 + lax.rem(z + dz, 8)

    x_copy = pltpu.make_async_copy(x_hbm, xv, local_sems.at[0])
    x_copy.start()
    d_copy = pltpu.make_async_copy(d_hbm, ext.at[pl.ds(BLK_DEV, BLK_DEV)], local_sems.at[1])
    d_copy.start()

    barrier = pltpu.get_barrier_semaphore()
    for n in (left, right):
        pl.semaphore_signal(barrier, inc=1, device_id=(n, me), device_id_type=MESH)
    for dy, dz in PEERS:
        pl.semaphore_signal(barrier, inc=1, device_id=(g, peer(dy, dz)), device_id_type=MESH)
    pl.semaphore_wait(barrier, 17)

    to_right = pltpu.make_async_remote_copy(
        d_hbm, ext.at[pl.ds(0, BLK_DEV)], halo_send.at[0], halo_recv.at[0],
        device_id=(right, me), device_id_type=MESH)
    to_left = pltpu.make_async_remote_copy(
        d_hbm, ext.at[pl.ds(2 * BLK_DEV, BLK_DEV)], halo_send.at[1], halo_recv.at[1],
        device_id=(left, me), device_id_type=MESH)
    to_right.start()
    to_left.start()

    def rows_of_batch(b, carry):
        first = jnp.int32(0)
        second = jnp.int32(0)
        count = jnp.int32(0)
        for e in range(ACT):
            block = act[e, g * ROWS + b]
            mine = ((block >> 3) & (ROWS - 1)) == me
            row = jnp.minimum(((block >> 7) - g + 1) & 15, 2) * BLK_DEV + (block & 7)
            first = jnp.where(mine & (count == 0), row, first)
            second = jnp.where(mine & (count == 1), row, second)
            count = count + mine.astype(jnp.int32)
        tab_row[2 * b] = first
        tab_row[2 * b + 1] = second
        tab_row[2 * ROWS + b] = count
        return carry

    lax.fori_loop(0, ROWS, rows_of_batch, 0)

    d_copy.wait()
    to_right.wait_recv()
    to_left.wait_recv()

    first_copies = []
    for i, (dy, dz) in enumerate(PEERS):
        p = peer(dy, dz)
        for c in range(2):
            send_d[p, c] = ext[tab_row[2 * p + c]]
        copy = pltpu.make_async_remote_copy(
            send_d.at[p], recv_d.at[pl.ds(2 * me, 2)], a2a_send.at[i], a2a_recv.at[i],
            device_id=(g, p), device_id_type=MESH)
        copy.start()
        first_copies.append(copy)
    for c in range(2):
        recv_d[2 * me + c] = ext[tab_row[2 * me + c]]

    ids = [act[k, g * ROWS + me] for k in range(ACT)]
    owners = [(i >> 3) & (ROWS - 1) for i in ids]
    for k in range(ACT):
        earlier = jnp.int32(0)
        for j in range(k):
            earlier = earlier + (owners[j] == owners[k]).astype(jnp.int32)
        tab_arr[k] = owners[k] * 2 + jnp.minimum(earlier, 1)

    def slot_entries(s, carry):
        entry = jnp.int32(0)
        for k in range(ACT):
            entry = jnp.where(tab_arr[k] == s, k, entry)
        tab_slot[s] = entry
        return carry

    lax.fori_loop(0, 2 * ROWS, slot_entries, 0)

    def match_row(k, carry):
        block = act[k, g * ROWS + me]
        found_m = [jnp.int32(KNZ)] * ACT
        for m in range(KNZ):
            column = pat[m, block]
            found = jnp.int32(ACT)
            for j in range(ACT):
                same = column == act[j, g * ROWS + me]
                found = jnp.where(same, j, found)
                found_m[j] = jnp.where(same, m, found_m[j])
            tab_j[k * KNZ + m] = found
        for j in range(ACT):
            tab_m[k * ACT + j] = found_m[j]
        return carry

    lax.fori_loop(0, ACT, match_row, 0)

    rows2[:, :, KNZ // 2] = jnp.zeros((2, ACT, BS, 128), BF16)
    hrows[:, :, ACT // 2] = jnp.zeros((2, ACT, BS, 128), BF16)
    recv_h[:, 2] = jnp.zeros((ROWS, BS, WIDTH), BF16)

    x_copy.wait()

    def transpose_chunk(i, carry):
        points = pl.ds(pl.multiple_of(i * 128, 128), 128)
        xt[:, points] = jnp.transpose(xv[points, :])
        return carry

    lax.fori_loop(0, PTS // 128, transpose_chunk, 0)

    masks = half_masks()
    for copy in first_copies:
        copy.wait_recv()

    def spread_row(k, carry):
        row = recv_d[tab_arr[k]]
        for q in range(KNZ // 2):
            part = row[:, q * 128 : (q + 1) * 128]
            rows2[0, k, q] = part
            rows2[1, k, q] = swap_halves(part.astype(F32)).astype(BF16)
        for q in range(ACT // 2):
            first = tab_m[k * ACT + 2 * q]
            second = tab_m[k * ACT + 2 * q + 1]
            dfull[pl.ds(pl.multiple_of(k * BS, BS), BS), q * 128 : (q + 1) * 128] = pair_of_blocks(
                rows2, k, first, second, masks)
        return carry

    lax.fori_loop(0, ACT, spread_row, 0)

    def density_chunk(i, carry):
        points = pl.ds(pl.multiple_of(i * CHUNK, CHUNK), CHUNK)
        x = xv[points, :]
        part = jnp.zeros((CHUNK, 128), F32)
        for n in range(COLS // CHUNK):
            product = jnp.dot(x, dfull[:, n * CHUNK : (n + 1) * CHUNK], preferred_element_type=F32)
            product = product * x[:, n * CHUNK : (n + 1) * CHUNK].astype(F32)
            part = part + (product[:, :128] + product[:, 128:])
        dens = jnp.sum(jnp.transpose(part), axis=0, keepdims=True)
        for half in range(CHUNK // 128):
            row = pl.ds(i * (CHUNK // 128) + half, 1)
            dens_half = dens[:, half * 128 : (half + 1) * 128]
            dens_out[row, :] = dens_half
            svec[:, pl.ds(pl.multiple_of(i * CHUNK + half * 128, 128), 128)] = weights[row, :] * jnp.tanh(dens_half)
        return carry

    lax.fori_loop(0, PTS // CHUNK, density_chunk, 0)

    def ham_chunk(i, carry):
        scaled = (xt[pl.ds(pl.multiple_of(i * CHUNK, CHUNK), CHUNK), :].astype(F32) * svec[...]).astype(BF16)
        for n in range(COLS // CHUNK):
            block = jnp.dot(scaled, xv[:, n * CHUNK : (n + 1) * CHUNK], preferred_element_type=F32)
            for half in range(CHUNK // 128):
                part = block[:, half * 128 : (half + 1) * 128]
                swapped = swap_halves(part).astype(BF16)
                part = part.astype(BF16)
                for kk in range(CHUNK // BS):
                    entry = i * (CHUNK // BS) + kk
                    hrows[0, entry, 2 * n + half] = part[kk * BS : (kk + 1) * BS]
                    hrows[1, entry, 2 * n + half] = swapped[kk * BS : (kk + 1) * BS]
        return carry

    lax.fori_loop(0, COLS // CHUNK, ham_chunk, 0)

    for copy in first_copies:
        copy.wait_send()

    def gather_slots(p, target, target_row):
        for c in range(2):
            k = tab_slot[2 * p + c]
            for q in range(KNZ // 2):
                first = tab_j[k * KNZ + 2 * q]
                second = tab_j[k * KNZ + 2 * q + 1]
                target[target_row, c, :, q * 128 : (q + 1) * 128] = pair_of_blocks(
                    hrows, k, first, second, masks)

    second_copies = []
    for i, (dy, dz) in enumerate(PEERS):
        p = peer(dy, dz)
        gather_slots(p, send_h, p)
        copy = pltpu.make_async_remote_copy(
            send_h.at[p], recv_h.at[me, pl.ds(0, 2)], a2a_send.at[15 + i], a2a_recv.at[15 + i],
            device_id=(g, p), device_id_type=MESH)
        copy.start()
        second_copies.append(copy)
    gather_slots(me, recv_h, me)
    for copy in second_copies:
        copy.wait_recv()

    def sum_row(t):
        picks = []
        for b in range(ROWS):
            count = tab_row[2 * ROWS + b]
            picks.append(jnp.where(
                (tab_row[2 * b] == t) & (count > 0), 0,
                jnp.where((tab_row[2 * b + 1] == t) & (count > 1), 1, 2)))
        total = recv_h[0, picks[0]].astype(F32)
        for b in range(1, ROWS):
            total = total + recv_h[b, picks[b]].astype(F32)
        return total

    def side_row(t, carry):
        for side, base in ((0, 0), (1, 2 * BLK_DEV)):
            halo_out[side, t] = sum_row(base + t).astype(BF16)
        return carry

    lax.fori_loop(0, BLK_DEV, side_row, 0)

    back_left = pltpu.make_async_remote_copy(
        halo_out.at[0], halo_in.at[0], halo_send.at[2], halo_recv.at[2],
        device_id=(left, me), device_id_type=MESH)
    back_right = pltpu.make_async_remote_copy(
        halo_out.at[1], halo_in.at[1], halo_send.at[3], halo_recv.at[3],
        device_id=(right, me), device_id_type=MESH)
    back_left.start()
    back_right.start()

    def own_row(t, carry):
        ham_out[t] = sum_row(BLK_DEV + t)
        return carry

    lax.fori_loop(0, BLK_DEV, own_row, 0)
    back_left.wait_recv()
    back_right.wait_recv()

    def add_row(t, carry):
        ham_out[t] = ham_out[t] + halo_in[0, t].astype(F32) + halo_in[1, t].astype(F32)
        return carry

    lax.fori_loop(0, BLK_DEV, add_row, 0)

    for copy in second_copies:
        copy.wait_send()
    for copy in (to_right, to_left, back_left, back_right):
        copy.wait_send()


def offset_of(i):
    i = lax.rem(i, 8) * 2 + lax.div(i, 8)
    j = lax.div(i, 2)
    dz = 4 + lax.div(j + 1, 2) * (1 - 2 * lax.rem(j, 2))
    return 1 - lax.rem(i, 2), dz


def fill_slot(slots, slot, source, pick, masks):
    low, high = masks
    for q in range(CAP // 2):
        slots[slot, q * BS : (q + 1) * BS] = two_blocks(source, *pick(2 * q), *pick(2 * q + 1), masks)
    row, block = pick(CAP - 1)
    a = source[block & 1, row, block >> 1]
    b = source[1 - (block & 1), row, block >> 1]
    half = BS // 2
    slots[slot, CAP // 2 * BS :] = a[:half] * low[:half] + b[half:] * high[half:]


def open_slot(target, slots, slot):
    for q in range(CAP // 2):
        keep_both(target, slot, q, slots[slot, q * BS : (q + 1) * BS])
    part = slots[slot, CAP // 2 * BS :]
    swapped = swap_halves(part.astype(F32)).astype(BF16)
    half = BS // 2
    target[0, slot, CAP // 2, :half] = part
    target[0, slot, CAP // 2, half:] = swapped
    target[1, slot, CAP // 2, :half] = swapped
    target[1, slot, CAP // 2, half:] = part


def packed_kernel(
    act, pat_hbm, weights, x_hbm, d_hbm,
    dens_out, ham_out, flag_out,
    xv, xt, own, halo_d, ext2, send_d, recv_d, rows2, dfull, svec, hrows, send_h,
    recv_h, hvar, expanded, halo_out, halo_in, row_flags, region_flags,
    pat, halo_src, row_map, back_map, tab_row, tab_src, tab_pos,
    tab_j, tab_rank, tab_local, tab_q, tab_start, tab_owner, tab_dpos, tab_h, tab_turn, tab_place, tab_order,
    local_sems, halo_send, halo_recv, a2a_send, a2a_recv, flag_send, flag_recv,
):
    g = lax.axis_index("region")
    me = lax.axis_index("rows")
    y = lax.div(me, 8)
    z = lax.rem(me, 8)
    left, right = lax.rem(g + 15, 16), lax.rem(g + 1, 16)

    def peer(i):
        dy, dz = offset_of(i)
        return lax.rem(y + dy, 2) * 8 + lax.rem(z + dz, 8)

    def sender(i):
        dy, dz = offset_of(i)
        return lax.rem(y + dy, 2) * 8 + lax.rem(z + 8 - dz, 8)

    x_copy = pltpu.make_async_copy(x_hbm, xv, local_sems.at[0])
    d_copy = pltpu.make_async_copy(d_hbm, own, local_sems.at[1])
    pat_copy = pltpu.make_async_copy(pat_hbm, pat, local_sems.at[2])
    d_copy.start()
    pat_copy.start()
    x_copy.start()

    barrier = pltpu.get_barrier_semaphore()
    for n in (left, right) + tuple(lax.rem(g + 16 - hop, 16) for hop in (2, 4, 8)):
        pl.semaphore_signal(barrier, inc=1, device_id=(n, me), device_id_type=MESH)

    def greet(i, carry):
        pl.semaphore_signal(barrier, inc=1, device_id=(g, peer(i)), device_id_type=MESH)
        return carry

    lax.fori_loop(0, ROWS - 1, greet, 0)

    def named(region, start):
        def one(b, mask):
            for e in range(start, start + 4):
                block = act[e, region * ROWS + b]
                bit = (1 + (block & 1)) * (1 + 3 * ((block >> 1) & 1)) * (1 + 15 * ((block >> 2) & 1))
                mask = mask | jnp.where(((block >> 3) & (ROWS - 1)) == me, bit, 0)
            return mask

        return lax.fori_loop(0, ROWS, one, jnp.int32(0))

    def ranks(mask):
        taken = jnp.int32(0)
        bits, places = [], []
        for s in range(BLK_DEV):
            bit = (mask >> s) & 1
            bits.append(bit)
            places.append(taken)
            taken = taken + bit
        return bits, places, taken

    overflow = jnp.int32(0)
    for side, mask in enumerate((named(right, 8), named(left, 12))):
        bits, places, taken = ranks(mask)
        for i in range(HALO):
            source = jnp.int32(0)
            for s in range(BLK_DEV):
                source = jnp.where((bits[s] == 1) & (places[s] == i), s, source)
            halo_src[side * HALO + i] = source
        for s in range(BLK_DEV):
            back_map[side * BLK_DEV + s] = jnp.where(bits[s] == 1, jnp.minimum(places[s], HALO - 1), HALO)
        overflow = jnp.maximum(overflow, (taken > HALO).astype(jnp.int32))

    d_copy.wait()
    for side in range(2):
        for i in range(HALO):
            halo_out[side, i] = own[halo_src[side * HALO + i]]
    pl.semaphore_wait(barrier, 20)

    to_right = pltpu.make_async_remote_copy(
        halo_out.at[0], halo_d.at[0], halo_send.at[0], halo_recv.at[0],
        device_id=(right, me), device_id_type=MESH)
    to_left = pltpu.make_async_remote_copy(
        halo_out.at[1], halo_d.at[1], halo_send.at[1], halo_recv.at[1],
        device_id=(left, me), device_id_type=MESH)
    to_right.start()
    to_left.start()

    for side, start in ((0, 8), (1, 12)):
        bits, places, taken = ranks(named(g, start))
        for s in range(BLK_DEV):
            row_map[2 * side * BLK_DEV + s] = side * (HALO + BLK_DEV) + jnp.minimum(places[s], HALO - 1)
    for s in range(BLK_DEV):
        row_map[BLK_DEV + s] = HALO + s

    def own_row_twice(s, carry):
        for q in range(KNZ // 2):
            keep_both(ext2, HALO + s, q, own[s, :, q * 128 : (q + 1) * 128])
        return carry

    lax.fori_loop(0, BLK_DEV, own_row_twice, 0)

    def batch_table(b):
        ids = [act[e, g * ROWS + b] for e in range(ACT)]
        blocks = [jnp.int32(0), jnp.int32(0)]
        count = jnp.int32(0)
        for e in range(ACT):
            mine = ((ids[e] >> 3) & (ROWS - 1)) == me
            blocks[0] = jnp.where(mine & (count == 0), ids[e], blocks[0])
            blocks[1] = jnp.where(mine & (count == 1), ids[e], blocks[1])
            count = count + mine.astype(jnp.int32)
        packed = [jnp.int32(0)] * CAP
        running = jnp.int32(0)
        for c in range(2):
            group = jnp.minimum(((blocks[c] >> 7) - g + 1) & 15, 2)
            tab_row[2 * b + c] = row_map[group * BLK_DEV + (blocks[c] & 7)]
            valid = count > c
            for m in range(KNZ):
                column = pat[m, blocks[c]]
                gap = column ^ ids[0]
                for e in range(1, ACT):
                    gap = jnp.minimum(gap, column ^ ids[e])
                match = (gap == 0) & valid
                for p in range(min(m + 1, CAP) if c == 0 else CAP):
                    packed[p] = jnp.where(match & (running == p), c * KNZ + m, packed[p])
                tab_pos[b * 16 + c * KNZ + m] = jnp.where(match, jnp.minimum(running, CAP - 1), KNZ)
                running = running + match.astype(jnp.int32)
        for p in range(CAP):
            tab_src[b * KNZ + p] = packed[p]
        tab_row[2 * ROWS + b] = count

    masks = half_masks()

    def pack_rows(b, target):
        def pick(p):
            code = tab_src[b * KNZ + p]
            return tab_row[2 * b + (code >> 3)], code & 7

        fill_slot(target, b, ext2, pick, masks)

    def first_copy(i):
        p = peer(i)
        return pltpu.make_async_remote_copy(
            send_d.at[p], recv_d.at[me], a2a_send.at[i], a2a_recv.at[i],
            device_id=(g, p), device_id_type=MESH)

    pat_copy.wait()
    for i in range(AHEAD):
        batch_table(peer(i))
    to_right.wait_recv()
    to_left.wait_recv()
    for side in range(2):
        for i in range(HALO):
            for q in range(KNZ // 2):
                keep_both(ext2, side * (HALO + BLK_DEV) + i, q, halo_d[side, i, :, q * 128 : (q + 1) * 128])

    def send_first(i, carry):
        pack_rows(peer(i), send_d)
        first_copy(i).start()
        return carry

    def send_and_prepare(i, carry):
        send_first(i, carry)
        batch_table(peer(i + AHEAD))
        return carry

    lax.fori_loop(0, ROWS - AHEAD, send_and_prepare, 0)
    lax.fori_loop(ROWS - AHEAD, ROWS - 1, send_first, 0)
    pack_rows(me, recv_d)

    def match_row(k, carry):
        block = act[k, g * ROWS + me]
        tab_owner[k] = (block >> 3) & (ROWS - 1)
        local = [jnp.int32(KNZ)] * ACT
        running = jnp.int32(0)
        for m in range(KNZ):
            column = pat[m, block]
            found = jnp.int32(ACT)
            for j in range(ACT):
                same = column == act[j, g * ROWS + me]
                found = jnp.where(same, j, found)
                local[j] = jnp.where(same, running, local[j])
            tab_j[k * KNZ + m] = found
            tab_rank[k * KNZ + m] = jnp.where(found < ACT, running, 64)
            running = running + (found < ACT).astype(jnp.int32)
        for j in range(ACT):
            tab_local[k * ACT + j] = local[j]
        tab_q[k] = running
        return carry

    lax.fori_loop(0, ACT, match_row, 0)

    def start_row(k, most):
        start = jnp.int32(0)
        for j in range(ACT):
            start = start + jnp.where((j < k) & (tab_owner[j] == tab_owner[k]), tab_q[j], 0)
        tab_start[k] = start
        for j in range(ACT):
            local = tab_local[k * ACT + j]
            tab_dpos[k * ACT + j] = jnp.where(local < KNZ, jnp.minimum(start + local, CAP - 1), KNZ)
        return jnp.maximum(most, start + tab_q[k])

    most = lax.fori_loop(0, ACT, start_row, jnp.int32(0))
    overflow = jnp.maximum(overflow, (most > CAP).astype(jnp.int32))

    row_flags[me] = jnp.full((8, 128), overflow, jnp.int32)

    def row_flag_copy(i):
        p = peer(i)
        return pltpu.make_async_remote_copy(
            row_flags.at[me], row_flags.at[me], flag_send.at[i], flag_recv.at[i],
            device_id=(g, p), device_id_type=MESH)

    def region_flag_copy(r):
        return pltpu.make_async_remote_copy(
            region_flags.at[0, r], region_flags.at[1, r], flag_send.at[15 + r], flag_recv.at[15 + r],
            device_id=(lax.rem(g + 2**r, 16), me), device_id_type=MESH)

    def merge_flags(r):
        region_flag_copy(r).wait_recv()
        merged = jnp.maximum(region_flags[0, r], region_flags[1, r])
        if r < 3:
            region_flags[0, r + 1] = merged
            region_flag_copy(r + 1).start()
        else:
            flag_out[0, 0] = merged[0, 0]

    def send_flag(i, carry):
        row_flag_copy(i).start()
        return carry

    lax.fori_loop(0, ROWS - 1, send_flag, 0)

    def turn_of(i, carry):
        tab_turn[peer(i)] = i
        return carry

    lax.fori_loop(0, ROWS, turn_of, 0)

    def place_of(k, carry):
        turn = tab_turn[tab_owner[k]]
        place = jnp.int32(0)
        for j in range(ACT):
            other = tab_turn[tab_owner[j]]
            place = place + ((other < turn) | ((other == turn) & (j < k))).astype(jnp.int32)
        tab_place[k] = place
        return carry

    lax.fori_loop(0, ACT, place_of, 0)

    def entry_at(n, carry):
        entry = jnp.int32(0)
        for k in range(ACT):
            entry = jnp.where(tab_place[k] == n, k, entry)
        tab_order[n] = entry
        return carry

    lax.fori_loop(0, ACT, entry_at, 0)

    def slot_table(r, carry):
        entries = [jnp.int32(0), jnp.int32(0)]
        count = jnp.int32(0)
        for k in range(ACT):
            mine = tab_owner[k] == r
            entries[0] = jnp.where(mine & (count == 0), k, entries[0])
            entries[1] = jnp.where(mine & (count == 1), k, entries[1])
            count = count + mine.astype(jnp.int32)
        packed = [jnp.int32(0)] * CAP
        for c in range(2):
            k = entries[c]
            start = jnp.where(count > c, tab_start[k], 64)
            for m in range(KNZ):
                place = start + tab_rank[k * KNZ + m]
                code = tab_place[k] * ACT + jnp.minimum(tab_j[k * KNZ + m], ACT - 1)
                for p in range(min(m + 1, CAP) if c == 0 else CAP):
                    packed[p] = jnp.where(place == p, code, packed[p])
        for p in range(CAP):
            tab_h[r * KNZ + p] = packed[p]
        return carry

    lax.fori_loop(0, ROWS, slot_table, 0)

    rows2[:, :, KNZ // 2] = jnp.zeros((2, ROWS, BS, 128), BF16)
    hvar[:, :, KNZ // 2] = jnp.zeros((2, ROWS, BS, 128), BF16)
    expanded[2 * ROWS] = jnp.zeros((KNZ // 2, BS, 128), BF16)
    for side in range(2):
        halo_in[side, HALO] = jnp.zeros((BS, WIDTH), BF16)

    x_copy.wait()

    def transpose_chunk(i, carry):
        points = pl.ds(pl.multiple_of(i * 128, 128), 128)
        xt[:, :, points] = jnp.transpose(xv[points, :]).reshape(ACT, BS, 128)
        return carry

    lax.fori_loop(0, PTS // 128, transpose_chunk, 0)

    def spread_slot(r):
        open_slot(rows2, recv_d, r)

    spread_slot(me)

    def take_first(i, carry):
        first_copy(i).wait_recv()
        spread_slot(sender(i))
        return carry

    lax.fori_loop(0, ROWS - 1, take_first, 0)

    def assemble_row(k, carry):
        owner = tab_owner[k]
        for q in range(ACT // 2):
            dfull[pl.ds(pl.multiple_of(k * BS, BS), BS), q * 128 : (q + 1) * 128] = pair_of_blocks(
                rows2, owner, tab_dpos[k * ACT + 2 * q], tab_dpos[k * ACT + 2 * q + 1], masks)
        return carry

    lax.fori_loop(0, ACT, assemble_row, 0)

    def density_chunk(i, carry):
        points = pl.ds(pl.multiple_of(i * POINTS, POINTS), POINTS)
        x = xv[points, :]
        part = jnp.zeros((POINTS, 128), F32)
        for n in range(COLS // CHUNK):
            product = jnp.dot(x, dfull[:, n * CHUNK : (n + 1) * CHUNK], preferred_element_type=F32)
            product = product * x[:, n * CHUNK : (n + 1) * CHUNK].astype(F32)
            part = part + (product[:, :128] + product[:, 128:])
        dens = jnp.sum(jnp.transpose(part), axis=0, keepdims=True)
        for half in range(POINTS // 128):
            row = pl.ds(i * (POINTS // 128) + half, 1)
            dens_half = dens[:, half * 128 : (half + 1) * 128]
            dens_out[row, :] = dens_half
            svec[:, pl.ds(pl.multiple_of(i * POINTS + half * 128, 128), 128)] = weights[row, :] * jnp.tanh(dens_half)
        return carry

    lax.fori_loop(0, PTS // POINTS, density_chunk, 0)

    def take_flag(i, carry):
        row_flag_copy(i).wait_recv()
        return carry

    lax.fori_loop(0, ROWS - 1, take_flag, 0)
    merged = row_flags[0]
    for r in range(1, ROWS):
        merged = jnp.maximum(merged, row_flags[r])
    region_flags[0, 0] = merged
    region_flag_copy(0).start()

    def pack_slot(r, target):
        def pick(p):
            code = tab_h[r * KNZ + p]
            return code >> 4, code & 15

        fill_slot(target, r, hrows, pick, masks)

    def second_copy(i):
        p = peer(i)
        return pltpu.make_async_remote_copy(
            send_h.at[p], recv_h.at[me], a2a_send.at[15 + i], a2a_recv.at[15 + i],
            device_id=(g, p), device_id_type=MESH)

    def send_second(i, carry):
        p = peer(i)
        pack_slot(p, send_h)
        second_copy(i).start()
        return carry

    def ham_chunk(i, carry):
        rows = [xt[tab_order[i * (CHUNK // BS) + n]] for n in range(CHUNK // BS)]
        scaled = (jnp.concatenate(rows, axis=0).astype(F32) * svec[...]).astype(BF16)
        for n in range(COLS // CHUNK):
            block = jnp.dot(scaled, xv[:, n * CHUNK : (n + 1) * CHUNK], preferred_element_type=F32)
            for half in range(CHUNK // 128):
                part = block[:, half * 128 : (half + 1) * 128]
                swapped = swap_halves(part).astype(BF16)
                part = part.astype(BF16)
                for kk in range(CHUNK // BS):
                    entry = i * (CHUNK // BS) + kk
                    hrows[0, entry, 2 * n + half] = part[kk * BS : (kk + 1) * BS]
                    hrows[1, entry, 2 * n + half] = swapped[kk * BS : (kk + 1) * BS]
        send_second(2 * i, 0)
        send_second(2 * i + 1, 0)
        return carry

    lax.fori_loop(0, COLS // CHUNK, ham_chunk, 0)
    lax.fori_loop(2 * (COLS // CHUNK), ROWS - 1, send_second, 0)
    pack_slot(me, recv_h)

    merge_flags(0)
    merge_flags(1)
    merge_flags(2)

    def expand_slot(b):
        open_slot(hvar, recv_h, b)
        for c in range(2):
            for q in range(KNZ // 2):
                expanded[2 * b + c, q] = pair_of_blocks(
                    hvar, b, tab_pos[b * 16 + c * KNZ + 2 * q], tab_pos[b * 16 + c * KNZ + 2 * q + 1], masks)

    expand_slot(me)

    def take_second(i, carry):
        second_copy(i).wait_recv()
        expand_slot(sender(i))
        return carry

    lax.fori_loop(0, ROWS - 1, take_second, 0)

    def sum_row(t):
        picks = []
        for b in range(ROWS):
            count = tab_row[2 * ROWS + b]
            picks.append(jnp.where(
                (tab_row[2 * b] == t) & (count > 0), 2 * b,
                jnp.where((tab_row[2 * b + 1] == t) & (count > 1), 2 * b + 1, 2 * ROWS)))
        total = expanded[picks[0]].astype(F32)
        for b in range(1, ROWS):
            total = total + expanded[picks[b]].astype(F32)
        return total

    to_right.wait_send()
    to_left.wait_send()

    def side_row(t, carry):
        for side in range(2):
            total = sum_row(side * (HALO + BLK_DEV) + t).astype(BF16)
            for q in range(KNZ // 2):
                halo_out[side, t, :, q * 128 : (q + 1) * 128] = total[q]
        return carry

    lax.fori_loop(0, HALO, side_row, 0)

    back_left = pltpu.make_async_remote_copy(
        halo_out.at[0], halo_in.at[0, pl.ds(0, HALO)], halo_send.at[2], halo_recv.at[2],
        device_id=(left, me), device_id_type=MESH)
    back_right = pltpu.make_async_remote_copy(
        halo_out.at[1], halo_in.at[1, pl.ds(0, HALO)], halo_send.at[3], halo_recv.at[3],
        device_id=(right, me), device_id_type=MESH)
    back_left.start()
    back_right.start()

    def own_row(t, carry):
        total = sum_row(HALO + t)
        for q in range(KNZ // 2):
            ham_out[t, :, q * 128 : (q + 1) * 128] = total[q]
        return carry

    lax.fori_loop(0, BLK_DEV, own_row, 0)
    merge_flags(3)
    back_left.wait_recv()
    back_right.wait_recv()

    def add_row(t, carry):
        ham_out[t] = (
            ham_out[t]
            + halo_in[0, back_map[t]].astype(F32)
            + halo_in[1, back_map[BLK_DEV + t]].astype(F32)
        )
        return carry

    lax.fori_loop(0, BLK_DEV, add_row, 0)

    def finish(i, carry):
        first_copy(i).wait_send()
        second_copy(i).wait_send()
        row_flag_copy(i).wait_send()
        return carry

    lax.fori_loop(0, ROWS - 1, finish, 0)
    for r in range(4):
        region_flag_copy(r).wait_send()
    back_left.wait_send()
    back_right.wait_send()


def specs():
    vmem = pl.BlockSpec(memory_space=pltpu.VMEM)
    smem = pl.BlockSpec(memory_space=pltpu.SMEM)
    hbm = pl.BlockSpec(memory_space=pl.ANY)
    return [smem, smem, vmem, hbm, hbm], vmem


def full_capacity(act, pat, weights, x, d):
    in_specs, vmem = specs()
    return pl.pallas_call(
        full_kernel,
        out_shape=(
            jax.ShapeDtypeStruct((PTS // 128, 128), F32),
            jax.ShapeDtypeStruct((BLK_DEV, BS, WIDTH), F32),
        ),
        in_specs=in_specs,
        out_specs=(vmem, vmem),
        scratch_shapes=[
            pltpu.VMEM((PTS, COLS), BF16),
            pltpu.VMEM((COLS, PTS), BF16),
            pltpu.VMEM((3 * BLK_DEV, BS, WIDTH), BF16),
            pltpu.VMEM((ROWS, 2, BS, WIDTH), BF16),
            pltpu.VMEM((2 * ROWS, BS, WIDTH), BF16),
            pltpu.VMEM((2, ACT, KNZ // 2 + 1, BS, 128), BF16),
            pltpu.VMEM((COLS, COLS), BF16),
            pltpu.VMEM((1, PTS), F32),
            pltpu.VMEM((2, ACT, ACT // 2 + 1, BS, 128), BF16),
            pltpu.VMEM((ROWS, 2, BS, WIDTH), BF16),
            pltpu.VMEM((ROWS, 3, BS, WIDTH), BF16),
            pltpu.VMEM((2, BLK_DEV, BS, WIDTH), BF16),
            pltpu.VMEM((2, BLK_DEV, BS, WIDTH), BF16),
            pltpu.SMEM((3 * ROWS,), jnp.int32),
            pltpu.SMEM((ACT,), jnp.int32),
            pltpu.SMEM((ACT * ACT,), jnp.int32),
            pltpu.SMEM((ACT * KNZ,), jnp.int32),
            pltpu.SMEM((2 * ROWS,), jnp.int32),
            pltpu.SemaphoreType.DMA((2,)),
            pltpu.SemaphoreType.DMA((4,)),
            pltpu.SemaphoreType.DMA((4,)),
            pltpu.SemaphoreType.DMA((30,)),
            pltpu.SemaphoreType.DMA((30,)),
        ],
        compiler_params=pltpu.CompilerParams(
            collective_id=1, has_side_effects=True, vmem_limit_bytes=56 << 20
        ),
    )(act, pat, weights, x, d)


def packed_capacity(act, pat, weights, x, d):
    in_specs, vmem = specs()
    half = KNZ // 2
    in_specs[1] = in_specs[3]
    return pl.pallas_call(
        packed_kernel,
        out_shape=(
            jax.ShapeDtypeStruct((PTS // 128, 128), F32),
            jax.ShapeDtypeStruct((BLK_DEV, BS, WIDTH), F32),
            jax.ShapeDtypeStruct((1, 1), jnp.int32),
        ),
        in_specs=in_specs,
        out_specs=(vmem, vmem, in_specs[0]),
        scratch_shapes=[
            pltpu.VMEM((PTS, COLS), BF16),
            pltpu.VMEM((ACT, BS, PTS), BF16),
            pltpu.VMEM((BLK_DEV, BS, WIDTH), BF16),
            pltpu.VMEM((2, HALO, BS, WIDTH), BF16),
            pltpu.VMEM((2, BLK_DEV + 2 * HALO, half, BS, 128), BF16),
            pltpu.VMEM((ROWS, CAP * BS // 2, 128), BF16),
            pltpu.VMEM((ROWS, CAP * BS // 2, 128), BF16),
            pltpu.VMEM((2, ROWS, half + 1, BS, 128), BF16),
            pltpu.VMEM((COLS, COLS), BF16),
            pltpu.VMEM((1, PTS), F32),
            pltpu.VMEM((2, ACT, ACT // 2, BS, 128), BF16),
            pltpu.VMEM((ROWS, CAP * BS // 2, 128), BF16),
            pltpu.VMEM((ROWS, CAP * BS // 2, 128), BF16),
            pltpu.VMEM((2, ROWS, half + 1, BS, 128), BF16),
            pltpu.VMEM((2 * ROWS + 1, half, BS, 128), BF16),
            pltpu.VMEM((2, HALO, BS, WIDTH), BF16),
            pltpu.VMEM((2, HALO + 1, BS, WIDTH), BF16),
            pltpu.VMEM((ROWS, 8, 128), jnp.int32),
            pltpu.VMEM((2, 4, 8, 128), jnp.int32),
            pltpu.SMEM((KNZ, NBLK), jnp.int32),
            pltpu.SMEM((2 * HALO,), jnp.int32),
            pltpu.SMEM((3 * BLK_DEV,), jnp.int32),
            pltpu.SMEM((2 * BLK_DEV,), jnp.int32),
            pltpu.SMEM((3 * ROWS,), jnp.int32),
            pltpu.SMEM((ROWS * KNZ,), jnp.int32),
            pltpu.SMEM((ROWS * 2 * KNZ,), jnp.int32),
            pltpu.SMEM((ACT * KNZ,), jnp.int32),
            pltpu.SMEM((ACT * KNZ,), jnp.int32),
            pltpu.SMEM((ACT * ACT,), jnp.int32),
            pltpu.SMEM((ACT,), jnp.int32),
            pltpu.SMEM((ACT,), jnp.int32),
            pltpu.SMEM((ACT,), jnp.int32),
            pltpu.SMEM((ACT * ACT,), jnp.int32),
            pltpu.SMEM((ROWS * KNZ,), jnp.int32),
            pltpu.SMEM((ROWS,), jnp.int32),
            pltpu.SMEM((ACT,), jnp.int32),
            pltpu.SMEM((ACT,), jnp.int32),
            pltpu.SemaphoreType.DMA((3,)),
            pltpu.SemaphoreType.DMA((4,)),
            pltpu.SemaphoreType.DMA((4,)),
            pltpu.SemaphoreType.DMA((30,)),
            pltpu.SemaphoreType.DMA((30,)),
            pltpu.SemaphoreType.DMA((19,)),
            pltpu.SemaphoreType.DMA((19,)),
        ],
        compiler_params=pltpu.CompilerParams(
            collective_id=0, has_side_effects=True, vmem_limit_bytes=56 << 20
        ),
    )(act, pat, weights, x, d)


def shards(basis_values, grid_weights, density_blocks, pattern, active):
    args = (
        active.T,
        pattern.T,
        grid_weights.reshape(PTS // 128, 128),
        basis_values,
        density_blocks.reshape(BLK_DEV, BS, WIDTH),
    )
    dens, ham, flag = packed_capacity(*args)
    dens, ham = lax.cond(flag[0, 0] > 0, lambda: tuple(full_capacity(*args)), lambda: (dens, ham))
    return dens.reshape(PTS), ham.reshape(BLK_DEV * BS, WIDTH)


def solution(mesh):
    placed = (
        P(("region", "rows"), None),
        P(("region", "rows")),
        P(("region", "rows"), None),
        P(),
        P(),
    )
    return jax.shard_map(
        shards,
        mesh=mesh,
        in_specs=placed,
        out_specs=(P(("region", "rows")), P(("region", "rows"), None)),
        check_vma=False,
    )
```
